128 devices in a mesh: gy: 8 (over x, z_lo), gz: 16 (over z_hi, y, core).
Axes of the slice: x: 4, y: 4, z: 4 (z_hi: 2, z_lo: 2; z = z_hi * 2 + z_lo), core: 2. Of those that a mesh axis runs over, the one named last changes fastest.
Arguments:
- forcing: bfloat16 [3, 256, 256, 256], P(None, 'gy', 'gz'), may hold values from -10.6 to 10.6
- lift_weight: bfloat16 [20, 3], replicated, may hold values from -3.5 to 3.5
- lift_bias: float32 [20], replicated, may hold values from -3 to 3
- point_weight: bfloat16 [20, 20], replicated, may hold values from -1.25 to 1.25
- spectral_weight: bfloat16 [64, 64, 20, 1280], P('gz', 'gy'), may hold values from -4 to 4
- mixing: float32 [20], replicated, may hold values from 0.3 to 1
- iterate: bfloat16 [20, 256, 256, 256], P(None, 'gy', 'gz'), may hold values from -14.2 to 14.2
- prev_iterate: bfloat16 [20, 256, 256, 256], P(None, 'gy', 'gz'), may hold values from -10.1 to 10.1
- prev_residual: bfloat16 [20, 256, 256, 256], P(None, 'gy', 'gz'), may hold values from -24.1 to 24.1
Outputs:
- next_residual: bfloat16 [20, 256, 256, 256], P(None, 'gy', 'gz')
- mixing_weights: float32 [2], replicated
The draws below stay inside these ranges and needn't reach their ends.
All inputs are finite; a program needn't handle non-finite values.
Results may differ from the reference program's by a relative error of at most 0.017.
Values may be sent and summed in bfloat16 or wider, within the bound.
A program may use at most 192 MiB of HBM per device.

```python
import math
import jax
import jax.numpy as jnp
from jax import lax

C = 20
MODES = 32
NX = 256
NY = 256
NZ = 256
KM = 64


def profile(strength):
    along_y = jnp.arange(NY, dtype=jnp.float32) / NY
    along_z = jnp.arange(NZ, dtype=jnp.float32) / NZ
    rising = jnp.exp(strength * (along_y[:, None] + 2.0 * along_z[None, :]) / 3.0)
    return rising[None, :, :, None]


def rise_along_z(strength):
    along_z = jnp.arange(NZ, dtype=jnp.float32) / NZ - 0.5
    return jnp.exp(strength * along_z)[None, None, :, None]


def rise_along_y(strength):
    along_y = jnp.arange(NY, dtype=jnp.float32) / NY - 0.5
    return jnp.exp(strength * along_y)[None, :, None, None]


def shared_base(key):
    return jnp.clip(jax.random.normal(key, (C, NY, NZ, NX), jnp.float32), -5.0, 5.0)


def rough_field(key, channels, strength):
    base = jnp.clip(jax.random.normal(key, (channels, NY, NZ, NX), jnp.float32), -5.0, 5.0)
    return base * profile(strength)


def draw_forcing(key, part):
    key = jax.random.fold_in(key, 5)
    return rough_field(key, 3, 0.7).astype(jnp.bfloat16)


def draw_iterate(key, part):
    base = shared_base(key)
    return (base * rise_along_z(1.61)).astype(jnp.bfloat16)


def draw_prev_iterate(key, part):
    key = jax.random.fold_in(key, 17)
    return rough_field(key, C, 0.7).astype(jnp.bfloat16)


def draw_prev_residual(key, part):
    base = shared_base(key)
    key = jax.random.fold_in(key, 23)
    noise = jnp.clip(jax.random.normal(key, (C, NY, NZ, NX), jnp.float32), -5.0, 5.0)
    return (-0.7 * base * rise_along_z(1.61) + noise * rise_along_y(1.61)).astype(jnp.bfloat16)


def steps_of(rng, dims, shards, smallest, high):
    def one(axis_at, parts):
        draws = jax.random.uniform(jax.random.fold_in(jax.random.fold_in(rng, 6), axis_at), (parts,), jnp.float32, smallest / len(shards), high / len(shards))
        return jnp.repeat(jnp.exp(draws), dims[axis_at] // parts).reshape((-1,) + (1,) * (len(dims) - axis_at - 1))

    level = one(*shards[0])
    for cut in shards[1:]:
        level = level * one(*cut)
    return level


def centred(rng, dims, spread, limit, cuts=(), kind=jnp.bfloat16):
    values = spread * jax.random.normal(rng, dims, jnp.float32)
    if cuts:
        values = values * steps_of(rng, dims, cuts, -0.22, 0.18)
    return jnp.clip(values, -limit, limit).astype(kind)


def setup_inputs(seed: int = 0) -> dict:
    streams_of = jax.random.split(jax.random.key(seed), 10)
    return {
        "forcing": draw_forcing(jax.random.fold_in(streams_of[9], 71), 0),
        "lift_weight": centred(streams_of[1], (C, 3), 3 ** -0.5, 3.5),
        "lift_bias": centred(streams_of[2], (C,), 0.5, 3.0, (), jnp.float32),
        "point_weight": centred(streams_of[3], (C, C), C ** -0.5, 1.25),
        "spectral_weight": centred(streams_of[4], (KM, KM, C, C * KM), 0.6, 4.0, ((0, 16), (1, 8))),
        "mixing": jnp.clip(jnp.exp(jax.random.uniform(streams_of[5], (C,), jnp.float32, math.log(0.3), math.log(1.0))), 0.3, 1.0),
        "iterate": draw_iterate(jax.random.fold_in(streams_of[9], 71), 0),
        "prev_iterate": draw_prev_iterate(jax.random.fold_in(streams_of[9], 71), 0),
        "prev_residual": draw_prev_residual(jax.random.fold_in(streams_of[9], 71), 0),
    }


REG = 1e-3
EPS = 1e-6


def dft_table(length):
    positions = jnp.arange(length, dtype=jnp.int32)[:, None]
    waves = jnp.arange(2 * MODES, dtype=jnp.int32)[None, :]
    wave_number = jnp.where(waves < MODES, waves, waves - MODES + 1)
    angles = ((positions * wave_number) % length).astype(jnp.float32) * (2.0 * math.pi / length)
    cosine_sine = jnp.where(waves < MODES, jnp.cos(angles), jnp.sin(angles))
    return cosine_sine.astype(jnp.bfloat16), (cosine_sine * (2.0 / length)).astype(jnp.bfloat16)


def cell(state_field, forcing_wide, lift_weight, lift_bias, point_weight, spectral_weight, tables):
    (ex_fwd, ex_inv), (ey_fwd, ey_inv), (ez_fwd, ez_inv) = tables
    highest = lax.Precision.HIGHEST
    ex_wide = ex_fwd.astype(jnp.float32)
    ez_wide = ez_fwd.astype(jnp.float32)

    def forward_one(channel_plane):
        along_x = jnp.einsum('yzx,xa->ayz', channel_plane.astype(jnp.float32), ex_wide, precision=highest).astype(jnp.bfloat16)
        along_x = lax.optimization_barrier(along_x)
        return jnp.einsum('ayz,zk->aky', along_x.astype(jnp.float32), ez_wide, precision=highest)

    stacked = lax.map(forward_one, state_field)
    packed = jnp.transpose(stacked, (1, 2, 0, 3)).astype(jnp.bfloat16)
    packed_y = jnp.einsum('akcy,yb->akcb', packed.astype(jnp.float32), ey_fwd.astype(jnp.float32), precision=highest).astype(jnp.bfloat16)
    modes_all = 2 * MODES
    mode_weights = spectral_weight.reshape(modes_all, modes_all, C, C, modes_all)
    mode_out = jnp.einsum('akocb,akcb->akob', mode_weights.astype(jnp.float32), packed_y.astype(jnp.float32), precision=highest).astype(jnp.bfloat16)
    back_y = jnp.einsum('akob,yb->akoy', mode_out.astype(jnp.float32), ey_inv.astype(jnp.float32), precision=highest).astype(jnp.bfloat16)
    field_wide = state_field.astype(jnp.float32)
    ez_back = ez_inv.astype(jnp.float32)
    ex_back = ex_inv.astype(jnp.float32)

    def inverse_one(pieces):
        channel_plane, weight_row, lift_row, bias_value = pieces
        z_side = jnp.einsum('aky,zk->ayz', channel_plane.astype(jnp.float32), ez_back, precision=highest).astype(jnp.bfloat16)
        z_side = lax.optimization_barrier(z_side)
        spectral = jnp.einsum('ayz,xa->yzx', z_side.astype(jnp.float32), ex_back, precision=highest)
        pointwise = jnp.einsum('c,cyzx->yzx', weight_row.astype(jnp.float32), field_wide, precision=highest)
        inject = jnp.einsum('j,jyzx->yzx', lift_row.astype(jnp.float32), forcing_wide, precision=highest) + bias_value
        return jax.nn.gelu(spectral + pointwise + inject)

    return lax.map(inverse_one, (jnp.transpose(back_y, (2, 0, 1, 3)), point_weight, lift_weight, lift_bias))


def reference(forcing, lift_weight, lift_bias, point_weight, spectral_weight, mixing, iterate, prev_iterate, prev_residual):
    tables = (dft_table(NX), dft_table(NY), dft_table(NZ))
    forcing_wide = forcing.astype(jnp.float32)
    first_out = cell(iterate, forcing_wide, lift_weight, lift_bias, point_weight, spectral_weight, tables)
    current = iterate.astype(jnp.float32)
    newest = first_out - current
    earlier = prev_residual.astype(jnp.float32)
    norm_old = jnp.sum(earlier * earlier)
    cross_term = jnp.sum(earlier * newest)
    norm_new = jnp.sum(newest * newest)
    ridge_term = REG * (norm_old + norm_new) + EPS
    denominator = norm_old + norm_new - 2.0 * cross_term + 2.0 * ridge_term
    weight_old = (norm_new + ridge_term - cross_term) / denominator
    weight_new = (norm_old + ridge_term - cross_term) / denominator
    damping = mixing[:, None, None, None]
    next_iterate = (weight_old * (prev_iterate.astype(jnp.float32) + damping * earlier) + weight_new * (current + damping * newest)).astype(jnp.bfloat16)
    second_out = cell(next_iterate, forcing_wide, lift_weight, lift_bias, point_weight, spectral_weight, tables)
    next_residual = (second_out - next_iterate.astype(jnp.float32)).astype(jnp.bfloat16)
    return next_residual, jnp.stack([weight_old, weight_new])
```

```python
import functools
import math

import jax
import jax.numpy as jnp
import ml_dtypes
import numpy as np
from jax import lax
from jax.experimental import pallas as pl
from jax.experimental.pallas import tpu as pltpu
from jax.sharding import PartitionSpec as P

MESH = pl.DeviceIdType.MESH
BF = jnp.bfloat16
F32 = jnp.float32

MODES = 32
KM = 64
REG = 0.001
EPS = 1e-06

C = 20
LEN = 256
NGY = 8
NQ = 8
NH = 2
RY = 32
RZ = 16
GROUPS = 4
GY = 8
BA = 4
BK = 8
ROWS = C * NH * BA
HALF = C * BA


def dft_table(length):
    positions = np.arange(length)[:, None]
    waves = np.arange(2 * MODES)[None, :]
    number = np.where(waves < MODES, waves, waves - MODES + 1)
    angles = (positions * number % length).astype(np.float32) * np.float32(2.0 * math.pi / length)
    both = np.where(waves < MODES, np.cos(angles), np.sin(angles)).astype(np.float32)
    inverse = (both * np.float32(2.0 / length)).astype(ml_dtypes.bfloat16)
    return both.astype(ml_dtypes.bfloat16), inverse


@functools.lru_cache(maxsize=None)
def tables():
    fwd, inv = dft_table(LEN)
    f = fwd.astype(np.float32)
    i = inv.astype(np.float32)
    order = np.arange(KM).reshape(NH, NQ, BA).transpose(1, 0, 2).reshape(-1)
    ex = f[:, order].T
    ix = i[:, order].T
    eye_y = np.eye(GY, dtype=np.float32)
    eye_k = np.eye(BK, dtype=np.float32)
    kz = np.einsum("hqzgk,yw->hqyzgwk", f.reshape(NH, NQ, RZ, NGY, BK), eye_y)
    kz = kz.reshape(NH, NQ * GY * RZ, NGY * GY * BK)
    kzi = np.einsum("hqzgk,yw->hgykqwz", i.reshape(NH, NQ, RZ, NGY, BK), eye_y)
    kzi = kzi.reshape(NH, NGY * GY * BK, NQ * GY * RZ)
    ky = np.einsum("yb,kj->ykjb", f, eye_k).reshape(LEN * BK, BK * KM)
    kyi = np.einsum("yb,kj->kbyj", i, eye_k).reshape(BK * KM, LEN * BK)
    return tuple(np.ascontiguousarray(t).astype(ml_dtypes.bfloat16) for t in (ex, ix, kz, kzi, ky, kyi))


def iota(shape, axis):
    return lax.broadcasted_iota(jnp.int32, shape, axis)


def dot(a, b):
    return jnp.dot(a, b, preferred_element_type=F32)


def dot_nt(a, b):
    return lax.dot_general(a, b, (((1,), (1,)), ((), ())), preferred_element_type=F32)


def swap_rows(first, second):
    low = iota(first.shape, 1) < BA
    return (
        jnp.where(low, first, pltpu.roll(second, BA, 1)),
        jnp.where(low, pltpu.roll(first, BA, 1), second),
    )


def swap_lanes(first, second):
    axis = first.ndim - 1
    low = iota(first.shape, axis) < 64
    return (
        jnp.where(low, first, pltpu.roll(second, 64, axis)),
        jnp.where(low, pltpu.roll(first, 64, axis), second),
    )


def gelu(x):
    inner = x * (math.sqrt(2.0 / math.pi) + (math.sqrt(2.0 / math.pi) * 0.044715) * (x * x))
    half = 0.5 * x
    return half + half * jnp.tanh(inner)


def kernel(
    forcing, lift_w, lift_b, point_w, spec_w, mixing, iterate, prev_it, prev_res,
    ex, ix, kz_all, kzi_all, ky_hbm, kyi_hbm,
    out, weights_out,
    v, pit, pres, step, forc, wts, lhs, xs, xr, bs, br, pf, ps, pr, gs, gr, hs, hg,
    kz, kzi, ky, kyi, qm, mo, osc, acc, ar1, ar2, ones,
    load_sem, in_sem, out_sem, loc_sem,
    xs_sem, xr_sem, bs_sem, br_sem, ps_sem, pr_sem, gs_sem, gr_sem, hs_sem, hr_sem, zs_sem, zr_sem,
    s1_sem, r1_sem, s2_sem, r2_sem,
):
    gy = lax.axis_index("gy")
    gz = lax.axis_index("gz")
    h = gz // NQ
    q = gz % NQ

    barrier = pltpu.get_barrier_semaphore()
    for off in range(1, 16):
        pl.semaphore_signal(barrier, inc=1, device_id=(gy, (gz + off) % 16), device_id_type=MESH)
    for off in range(1, NGY):
        pl.semaphore_signal(barrier, inc=1, device_id=((gy + off) % NGY, gz), device_id_type=MESH)

    in_copies = [
        pltpu.make_async_copy(
            iterate.at[:, pl.ds(g * GY, GY)], v.at[:, pl.ds(g * GY, GY)], in_sem.at[g]
        )
        for g in range(GROUPS)
    ]
    loads = {
        name: pltpu.make_async_copy(src, dst, load_sem.at[n])
        for n, (name, src, dst) in enumerate([
            ("kz", kz_all.at[h], kz),
            ("ky", ky_hbm, ky),
            ("wts", spec_w, wts),
            ("kyi", kyi_hbm, kyi),
            ("kzi", kzi_all.at[h], kzi),
            ("forc", forcing, forc),
            ("pres", prev_res, pres),
            ("pit", prev_it, pit),
        ])
    }
    for copy in in_copies:
        copy.start()
    for copy in loads.values():
        copy.start()

    def send_x(g, off):
        dest = (q + off) % NQ
        return pltpu.make_async_remote_copy(
            xs.at[g, dest], xr.at[g, q], xs_sem.at[g, off], xr_sem.at[g, off],
            device_id=(gy, h * NQ + dest), device_id_type=MESH)

    def send_b(g, off):
        dest = (q + off) % NQ
        return pltpu.make_async_remote_copy(
            bs.at[g, dest], br.at[g, q], bs_sem.at[g, off], br_sem.at[g, off],
            device_id=(gy, h * NQ + dest), device_id_type=MESH)

    partner = (gy, (1 - h) * NQ + q)

    def send_p(g):
        return pltpu.make_async_remote_copy(
            ps.at[g, 1 - h], pr.at[g], ps_sem.at[g], pr_sem.at[g],
            device_id=partner, device_id_type=MESH)

    def send_z(p):
        return pltpu.make_async_remote_copy(
            hg.at[p, h], hg.at[p, h], zs_sem.at[p], zr_sem.at[p],
            device_id=partner, device_id_type=MESH)

    def recv_z(p):
        return pltpu.make_async_remote_copy(
            hg.at[p, h], hg.at[p, 1 - h], zs_sem.at[p], zr_sem.at[p],
            device_id=partner, device_id_type=MESH)

    def send_g(p, off):
        dest = (gy + off) % NGY
        return pltpu.make_async_remote_copy(
            gs.at[p, dest], gr.at[p, gy], gs_sem.at[p, off], gr_sem.at[p, off],
            device_id=(dest, gz), device_id_type=MESH)

    def send_h(p, off):
        dest = (gy + off) % NGY
        return pltpu.make_async_remote_copy(
            hs.at[p, dest], hg.at[p, h, gy], hs_sem.at[p, off], hr_sem.at[p, off],
            device_id=(dest, gz), device_id_type=MESH)

    def own_x(g):
        return pltpu.make_async_copy(xs.at[g, q], xr.at[g, q], loc_sem.at[g])

    def own_b(g):
        return pltpu.make_async_copy(bs.at[g, q], br.at[g, q], loc_sem.at[4 + g])

    def own_g(p):
        return pltpu.make_async_copy(gs.at[p, gy], gr.at[p, gy], loc_sem.at[8 + p])

    def own_h(p):
        return pltpu.make_async_copy(hs.at[p, gy], hg.at[p, h, gy], loc_sem.at[10 + p])

    def x_stage(g):
        for pair in range(C // 2):
            parts = []
            for j in range(2):
                field = v[2 * pair + j, pl.ds(g * GY, GY)].reshape(GY * RZ, LEN)
                parts.append(dot_nt(ex[...], field).reshape(NQ, NH * BA, GY * RZ))
            xs[g, :, pair * 16:(pair + 1) * 16, :] = jnp.concatenate(parts, axis=1).astype(BF)

    def z_stage(g):
        left = jnp.concatenate([xr[g, s] for s in range(NQ)], axis=1)
        part = dot(left, kz[...]).reshape(C // 2, 2, 8, 512)
        zero, one = swap_rows(part[:, 0], part[:, 1])
        zero = zero.reshape(HALF, 512)
        one = one.reshape(HALF, 512)
        pf[g, 0] = zero
        pf[g, 1] = one
        ps[g, 0] = zero.astype(BF)
        ps[g, 1] = one.astype(BF)

    def join_stage(p):
        first = pf[2 * p, h] + pr[2 * p].astype(F32)
        second = pf[2 * p + 1, h] + pr[2 * p + 1].astype(F32)
        for j in range(4):
            cut = slice(j * 128, (j + 1) * 128)
            even, odd = swap_lanes(first[:, cut], second[:, cut])
            gs[p, 2 * j] = even.astype(BF)
            gs[p, 2 * j + 1] = odd.astype(BF)

    def y_stage():
        left = jnp.concatenate([gr[p, s] for s in range(NGY) for p in range(2)], axis=1)
        modes = dot(left, ky[...]).astype(BF).astype(F32).reshape(C // 2, 8, 512)
        for m in range(4):
            here = modes[:, :, m * 128:(m + 1) * 128]
            there = pltpu.roll(here, BA, 1)
            even, odd = swap_lanes(here, there)
            qm[2 * m] = even
            qm[2 * m + 1] = odd

    def mix_stage():
        def one_pair(m, carry):
            for a in range(BA):
                sums = []
                for j in range(2):
                    k = 2 * m + j
                    total = jnp.zeros((C, 128), F32)
                    for t in range(C // 2):
                        w = wts[a, k, :, t * 128:(t + 1) * 128].astype(F32)
                        total = total + w * qm[k, t, a:a + 1, :]
                    sums.append(total + pltpu.roll(total, 64, 1))
                low = iota((C, 128), 1) < 64
                mo[m, pl.ds(a, C, stride=BA), :] = jnp.where(low, sums[0], sums[1])
            return carry

        lax.fori_loop(0, 4, one_pair, 0)

    def yi_stage():
        left = jnp.concatenate([mo[m].astype(BF) for m in range(4)], axis=1)
        for s in range(NGY):
            back = dot(left, kyi[:, s * 256:(s + 1) * 256]).astype(BF)
            hs[0, s] = back[:, :128]
            hs[1, s] = back[:, 128:]

    def zi_stage(p):
        cuts = {}
        for half in range(NH):
            for j in range(4):
                one = hg[p, half, 2 * j].astype(F32)
                two = hg[p, half, 2 * j + 1].astype(F32)
                cuts[half, j] = swap_lanes(one, two)
        for e in range(2):
            zero = jnp.concatenate([cuts[0, j][e] for j in range(4)], axis=1).reshape(C // 2, 8, 512)
            one = jnp.concatenate([cuts[1, j][e] for j in range(4)], axis=1).reshape(C // 2, 8, 512)
            even, odd = swap_rows(zero, one)
            left = jnp.concatenate([even, odd], axis=1).reshape(ROWS, 512).astype(BF)
            for s in range(0, NQ, 2):
                back = dot(left, kzi[:, s * 128:(s + 2) * 128]).astype(BF)
                bs[2 * p + e, s] = back[:, :128]
                bs[2 * p + e, s + 1] = back[:, 128:]

    def build_lhs():
        rows_o = iota((C * RZ, C), 0) // RZ
        pick = jnp.where(rows_o == iota((C * RZ, C), 1), 1.0, 0.0).astype(BF)
        col = iota((C, C * RZ), 1) // RZ
        spread = jnp.where(col == iota((C, C * RZ), 0), 1.0, 0.0).astype(BF)
        wide = dot(dot(pick, point_w[...]).astype(BF), spread)
        same = iota((C * RZ, C * RZ), 0) % RZ == iota((C * RZ, C * RZ), 1) % RZ
        wide = jnp.where(same, wide, 0.0)
        col3 = iota((3, 3 * RZ), 1) // RZ
        spread3 = jnp.where(col3 == iota((3, 3 * RZ), 0), 1.0, 0.0).astype(BF)
        lift = dot(dot(pick, lift_w[...]).astype(BF), spread3)
        same3 = iota((C * RZ, 3 * RZ), 0) % RZ == iota((C * RZ, 3 * RZ), 1) % RZ
        lift = jnp.where(same3, lift, 0.0)
        bias = lift_b[...]
        hi = bias.astype(BF).astype(F32)
        mid = (bias - hi).astype(BF).astype(F32)
        lo = (bias - hi - mid).astype(BF).astype(F32)
        row = iota((16, C), 0)
        pieces = jnp.where(row == 0, hi, jnp.where(row == 1, mid, jnp.where(row == 2, lo, 0.0)))
        bias_cols = dot_nt(pick, pieces.astype(BF))
        full = jnp.concatenate([wide, lift, bias_cols], axis=1).astype(BF)
        for y in range(GY):
            lhs[y, :, 0:384] = full
        ones[...] = jnp.ones((16, LEN), BF)

    def turn_stage(g):
        for pair in range(C // 2):
            tile = br[g, :, pair * 16:(pair + 1) * 16, :].astype(F32)
            for j in range(2):
                block = tile[:, 8 * j:8 * j + 8].reshape(KM, GY * RZ)
                turned = jnp.transpose(block, (1, 0)).astype(BF).reshape(GY, RZ, KM)
                o = 2 * pair + j
                lhs[:, o * RZ:(o + 1) * RZ, 384:448] = turned

    def field_row(y):
        return v[:, y].reshape(C * RZ, LEN)

    def pre_activation(yl, y):
        right = jnp.concatenate(
            [field_row(y), forc[:, y].reshape(3 * RZ, LEN), ones[...], ix[...]], axis=0)
        osc[...] = dot(lhs[yl][:, :448], right)

    def final_first(g):
        turn_stage(g)

        def row(yl, carry):
            y = g * GY + yl
            pre_activation(yl, y)
            s_oo = jnp.zeros((RZ, LEN), F32)
            s_on = jnp.zeros((RZ, LEN), F32)
            s_nn = jnp.zeros((RZ, LEN), F32)
            for o in range(C):
                current = v[o, y].astype(F32)
                earlier = pres[o, y].astype(F32)
                newest = gelu(osc[o * RZ:(o + 1) * RZ, :]) - current
                step[o, y] = current + mixing[o] * newest
                s_oo += earlier * earlier
                s_on += earlier * newest
                s_nn += newest * newest
            acc[0] += s_oo
            acc[1] += s_on
            acc[2] += s_nn
            return carry

        lax.fori_loop(0, GY, row, 0)

    def final_second(g):
        turn_stage(g)

        def row(yl, carry):
            y = g * GY + yl
            pre_activation(yl, y)
            for o in range(C):
                current = v[o, y].astype(F32)
                pres[o, y] = (gelu(osc[o * RZ:(o + 1) * RZ, :]) - current).astype(BF)
            return carry

        lax.fori_loop(0, GY, row, 0)

    def combine(g, w_old, w_new):
        def one(c, carry):
            ys = pl.ds(g * GY, GY)
            old = pit[c, ys].astype(F32) + mixing[c] * pres[c, ys].astype(F32)
            v[c, ys] = (w_old * old + w_new * step[c, ys]).astype(BF)
            return carry

        lax.fori_loop(0, C, one, 0)

    def cell(number, w_old=None, w_new=None):
        first = number == 0
        for g in range(GROUPS):
            if first:
                in_copies[g].wait()
            else:
                combine(g, w_old, w_new)
            x_stage(g)
            if first and g == 0:
                pl.semaphore_wait(barrier, 22)
            for off in range(1, NQ):
                send_x(g, off).start()
            own_x(g).start()
        if first:
            acc[...] = jnp.zeros((3, RZ, LEN), F32)
            build_lhs()
            loads["kz"].wait()

        def z_part(g):
            own_x(g).wait()
            for off in range(1, NQ):
                send_x(g, off).wait_recv()
            z_stage(g)
            send_p(g).start()

        def join_part(p):
            send_p(2 * p).wait_recv()
            send_p(2 * p + 1).wait_recv()
            join_stage(p)
            for off in range(1, NGY):
                send_g(p, off).start()
            own_g(p).start()

        z_part(0)
        z_part(1)
        z_part(2)
        join_part(0)
        z_part(3)
        join_part(1)
        if first:
            for name in ("ky", "wts", "kyi", "kzi", "forc", "pres"):
                loads[name].wait()
        for p in range(2):
            own_g(p).wait()
            for off in range(1, NGY):
                send_g(p, off).wait_recv()
        y_stage()
        mix_stage()
        yi_stage()
        for p in range(2):
            for off in range(1, NGY):
                send_h(p, off).start()
            own_h(p).start()
        for p in range(2):
            own_h(p).wait()
            for off in range(1, NGY):
                send_h(p, off).wait_recv()
            send_z(p).start()
        for p in range(2):
            recv_z(p).wait_recv()
            zi_stage(p)
            for g in (2 * p, 2 * p + 1):
                for off in range(1, NQ):
                    send_b(g, off).start()
                own_b(g).start()
        for g in range(GROUPS):
            own_b(g).wait()
            for off in range(1, NQ):
                send_b(g, off).wait_recv()
            if first:
                final_first(g)
            else:
                final_second(g)
                ys = pl.ds(g * GY, GY)
                pltpu.make_async_copy(pres.at[:, ys], out.at[:, ys], out_sem.at[g]).start()
        for g in range(GROUPS):
            for off in range(1, NQ):
                send_x(g, off).wait_send()
                send_b(g, off).wait_send()
            send_p(g).wait_send()
        for p in range(2):
            send_z(p).wait_send()
            for off in range(1, NGY):
                send_g(p, off).wait_send()
                send_h(p, off).wait_send()

    def reduce_norms():
        rows = iota((8, 128), 0)
        mine = jnp.zeros((8, 128), F32)
        for n in range(3):
            total = jnp.sum(acc[n], axis=0, keepdims=True)
            mine = jnp.where(rows == n, total[:, :128] + total[:, 128:], mine)
        ar1[gz] = mine
        sends = [
            pltpu.make_async_remote_copy(
                ar1.at[gz], ar1.at[gz], s1_sem.at[off], r1_sem.at[off],
                device_id=(gy, (gz + off) % 16), device_id_type=MESH)
            for off in range(1, 16)
        ]
        for copy in sends:
            copy.start()
        for off in range(1, 16):
            src = (gz - off + 16) % 16
            pltpu.make_async_remote_copy(
                ar1.at[gz], ar1.at[src], s1_sem.at[off], r1_sem.at[off],
                device_id=(gy, src), device_id_type=MESH).wait_recv()
        total = ar1[0]
        for s in range(1, 16):
            total = total + ar1[s]
        ar2[gy] = total
        sends2 = [
            pltpu.make_async_remote_copy(
                ar2.at[gy], ar2.at[gy], s2_sem.at[off], r2_sem.at[off],
                device_id=((gy + off) % NGY, gz), device_id_type=MESH)
            for off in range(1, NGY)
        ]
        for copy in sends2:
            copy.start()
        for off in range(1, NGY):
            src = (gy - off + NGY) % NGY
            pltpu.make_async_remote_copy(
                ar2.at[gy], ar2.at[src], s2_sem.at[off], r2_sem.at[off],
                device_id=(src, gz), device_id_type=MESH).wait_recv()
        total = ar2[0]
        for s in range(1, NGY):
            total = total + ar2[s]
        for copy in sends + sends2:
            copy.wait_send()
        sums = jnp.sum(total, axis=1, keepdims=True)
        norm_old, cross, norm_new = sums[0:1], sums[1:2], sums[2:3]
        ridge = REG * (norm_old + norm_new) + EPS
        denominator = norm_old + norm_new - 2.0 * cross + 2.0 * ridge
        w_old = (norm_new + ridge - cross) / denominator
        w_new = (norm_old + ridge - cross) / denominator
        lane = iota((8, 128), 1)
        weights_out[...] = jnp.where(lane == 0, w_old, w_new)
        return w_old.reshape(1, 1, 1), w_new.reshape(1, 1, 1)

    cell(0)
    w_old, w_new = reduce_norms()
    loads["pit"].wait()
    cell(1, w_old, w_new)
    for g in range(GROUPS):
        ys = pl.ds(g * GY, GY)
        pltpu.make_async_copy(pres.at[:, ys], out.at[:, ys], out_sem.at[g]).wait()


def shards(forcing, lift_weight, lift_bias, point_weight, spectral_weight, mixing, iterate, prev_iterate, prev_residual):
    ex, ix, kz, kzi, ky, kyi = (jnp.asarray(t) for t in tables())
    field = (C, RY, RZ, LEN)
    vmem = pl.BlockSpec(memory_space=pltpu.VMEM)
    smem = pl.BlockSpec(memory_space=pltpu.SMEM)
    hbm = pl.BlockSpec(memory_space=pl.ANY)
    dma = pltpu.SemaphoreType.DMA
    scratch = [
        pltpu.VMEM(field, BF),
        pltpu.VMEM(field, BF),
        pltpu.VMEM(field, BF),
        pltpu.VMEM(field, F32),
        pltpu.VMEM((3, RY, RZ, LEN), BF),
        pltpu.VMEM((BA, BK, C, C * KM), BF),
        pltpu.VMEM((GY, C * RZ, 512), BF),
        pltpu.VMEM((GROUPS, NQ, ROWS, 128), BF),
        pltpu.VMEM((GROUPS, NQ, ROWS, 128), BF),
        pltpu.VMEM((GROUPS, NQ, ROWS, 128), BF),
        pltpu.VMEM((GROUPS, NQ, ROWS, 128), BF),
        pltpu.VMEM((GROUPS, NH, HALF, 512), F32),
        pltpu.VMEM((GROUPS, NH, HALF, 512), BF),
        pltpu.VMEM((GROUPS, HALF, 512), BF),
        pltpu.VMEM((2, NGY, HALF, 128), BF),
        pltpu.VMEM((2, NGY, HALF, 128), BF),
        pltpu.VMEM((2, NGY, HALF, 128), BF),
        pltpu.VMEM((2, NH, NGY, HALF, 128), BF),
        pltpu.VMEM((1024, 512), BF),
        pltpu.VMEM((512, 1024), BF),
        pltpu.VMEM((2048, 512), BF),
        pltpu.VMEM((512, 2048), BF),
        pltpu.VMEM((BK, C // 2, 8, 128), F32),
        pltpu.VMEM((4, HALF, 128), F32),
        pltpu.VMEM((C * RZ, LEN), F32),
        pltpu.VMEM((3, RZ, LEN), F32),
        pltpu.VMEM((16, 8, 128), F32),
        pltpu.VMEM((NGY, 8, 128), F32),
        pltpu.VMEM((16, LEN), BF),
        dma((8,)), dma((GROUPS,)), dma((GROUPS,)), dma((12,)),
        dma((GROUPS, NQ)), dma((GROUPS, NQ)), dma((GROUPS, NQ)), dma((GROUPS, NQ)),
        dma((GROUPS,)), dma((GROUPS,)),
        dma((2, NGY)), dma((2, NGY)), dma((2, NGY)), dma((2, NGY)),
        dma((2,)), dma((2,)),
        dma((16,)), dma((16,)), dma((NGY,)), dma((NGY,)),
    ]
    result, weights = pl.pallas_call(
        kernel,
        out_shape=(
            jax.ShapeDtypeStruct(field, BF),
            jax.ShapeDtypeStruct((8, 128), F32),
        ),
        in_specs=[hbm, vmem, vmem, vmem, hbm, smem, hbm, hbm, hbm, vmem, vmem, hbm, hbm, hbm, hbm],
        out_specs=(hbm, vmem),
        scratch_shapes=scratch,
        compiler_params=pltpu.CompilerParams(
            collective_id=0, has_side_effects=True, vmem_limit_bytes=60 * 1024 * 1024),
        cost_estimate=pl.CostEstimate(
            flops=10_000_000_000, bytes_accessed=40_000_000, transcendentals=5_000_000),
    )(forcing, lift_weight, lift_bias.reshape(1, C), point_weight, spectral_weight, mixing,
      iterate, prev_iterate, prev_residual, ex, ix, kz, kzi, ky, kyi)
    return result, weights[0, :2]


def solution(mesh):
    in_specs = (
        P(None, "gy", "gz", None),
        P(),
        P(),
        P(),
        P("gz", "gy", None, None),
        P(),
        P(None, "gy", "gz", None),
        P(None, "gy", "gz", None),
        P(None, "gy", "gz", None),
    )
    out_specs = (P(None, "gy", "gz", None), P())
    return jax.shard_map(shards, mesh=mesh, in_specs=in_specs, out_specs=out_specs, check_vma=False)
```

```python
import functools
import math

import jax
import jax.numpy as jnp
import ml_dtypes
import numpy as np
from jax import lax
from jax.experimental import pallas as pl
from jax.experimental.pallas import tpu as pltpu
from jax.sharding import PartitionSpec as P

MESH = pl.DeviceIdType.MESH
BF = jnp.bfloat16
F32 = jnp.float32

MODES = 32
KM = 64
REG = 0.001
EPS = 1e-06

C = 20
LEN = 256
NGY = 8
NQ = 8
NH = 2
RY = 32
RZ = 16
GROUPS = 4
GY = 8
BA = 4
BK = 8
ROWS = C * NH * BA
HALF = C * BA


PEERS = [(dh, off) for off in range(NGY) for dh in range(NH) if (dh, off) != (0, 0)]


def dft_table(length):
    positions = np.arange(length)[:, None]
    waves = np.arange(2 * MODES)[None, :]
    number = np.where(waves < MODES, waves, waves - MODES + 1)
    angles = (positions * number % length).astype(np.float32) * np.float32(2.0 * math.pi / length)
    both = np.where(waves < MODES, np.cos(angles), np.sin(angles)).astype(np.float32)
    inverse = (both * np.float32(2.0 / length)).astype(ml_dtypes.bfloat16)
    return both.astype(ml_dtypes.bfloat16), inverse


@functools.lru_cache(maxsize=None)
def tables():
    fwd, inv = dft_table(LEN)
    f = fwd.astype(np.float32)
    i = inv.astype(np.float32)
    order = np.arange(KM).reshape(NH, NQ, BA).transpose(1, 0, 2).reshape(-1)
    ex = f[:, order].T
    ix = i[:, order].T
    eye_y = np.eye(GY, dtype=np.float32)
    eye_k = np.eye(BK, dtype=np.float32)
    kz = np.einsum("hqzgk,yw->hqyzgwk", f.reshape(NH, NQ, RZ, NGY, BK), eye_y)
    kz = kz.reshape(NH, NQ * GY * RZ, NGY * GY * BK)
    kzi = np.einsum("hqzgk,yw->hgykqwz", i.reshape(NH, NQ, RZ, NGY, BK), eye_y)
    kzi = kzi.reshape(NH, NGY * GY * BK, NQ * GY * RZ)
    ky = np.einsum("yb,kj->ykjb", f, eye_k).reshape(LEN * BK, BK * KM)
    kyi = np.einsum("yb,kj->kbyj", i, eye_k).reshape(BK * KM, LEN * BK)
    return tuple(np.ascontiguousarray(t).astype(ml_dtypes.bfloat16) for t in (ex, ix, kz, kzi, ky, kyi))


def iota(shape, axis):
    return lax.broadcasted_iota(jnp.int32, shape, axis)


def dot(a, b):
    return jnp.dot(a, b, preferred_element_type=F32)


def dot_nt(a, b):
    return lax.dot_general(a, b, (((1,), (1,)), ((), ())), preferred_element_type=F32)


def peer(place, off, ring):
    return (place // 2 + off // 2) % ring * 2 + (place + off) % 2


def swap_rows(first, second):
    low = iota(first.shape, 1) < BA
    return (
        jnp.where(low, first, pltpu.roll(second, BA, 1)),
        jnp.where(low, pltpu.roll(first, BA, 1), second),
    )


def swap_lanes(first, second):
    axis = first.ndim - 1
    low = iota(first.shape, axis) < 64
    return (
        jnp.where(low, first, pltpu.roll(second, 64, axis)),
        jnp.where(low, pltpu.roll(first, 64, axis), second),
    )


def gelu(x):
    inner = x * (math.sqrt(2.0 / math.pi) + (math.sqrt(2.0 / math.pi) * 0.044715) * (x * x))
    half = 0.5 * x
    return half + half * jnp.tanh(inner)


def kernel(
    forcing, lift_w, lift_b, point_w, spec_w, mixing, iterate, prev_it, prev_res,
    ex, ix, kz_all, kzi_all, ky_hbm, kyi_hbm,
    out, weights_out,
    v, pit, pres, step, forc, wts, lhs, xs, xr, xra, bs, br, pf, gs, gr, gsa, gra, hs, hg,
    kz, kzi, ky, kyi, qm, qt, qa, mo, osc, acc, ar1, ar2, ones,
    load_sem, in_sem, out_sem, loc_sem,
    xs_sem, xr_sem, xas_sem, xar_sem, bs_sem, br_sem, gs_sem, gr_sem, gas_sem, gar_sem, hs_sem, hr_sem,
    s1_sem, r1_sem, s2_sem, r2_sem,
):
    gy = lax.axis_index("gy")
    gz = lax.axis_index("gz")
    h = gz // NQ
    q = gz % NQ

    barrier = pltpu.get_barrier_semaphore()
    for off in range(1, 16):
        pl.semaphore_signal(barrier, inc=1, device_id=(gy, (gz + off) % 16), device_id_type=MESH)
    for dh, off in PEERS:
        if off:
            pl.semaphore_signal(
                barrier, inc=1, device_id=(peer(gy, off, NGY // 2), (h + dh) % NH * NQ + q),
                device_id_type=MESH)

    in_copies = [
        pltpu.make_async_copy(
            iterate.at[:, pl.ds(g * GY, GY)], v.at[:, pl.ds(g * GY, GY)], in_sem.at[g]
        )
        for g in range(GROUPS)
    ]
    loads = {
        name: pltpu.make_async_copy(src, dst, load_sem.at[n])
        for n, (name, src, dst) in enumerate([
            ("kz", kz_all.at[h], kz),
            ("pres", prev_res, pres),
            ("pit", prev_it, pit),
            ("ky", ky_hbm, ky),
            ("wts", spec_w, wts),
            ("kyi", kyi_hbm, kyi),
            ("kzi", kzi_all.at[h], kzi),
            ("forc", forcing, forc),
        ])
    }
    for copy in in_copies:
        copy.start()
    for copy in loads.values():
        copy.start()

    def to_q(src, dst, send_sem, recv_sem):
        def one(g, off):
            dest = peer(q, off, NQ // 2)
            return pltpu.make_async_remote_copy(
                src.at[g, dest], dst.at[g, q], send_sem.at[g, off], recv_sem.at[g, off],
                device_id=(gy, h * NQ + dest), device_id_type=MESH)
        return one

    send_x = to_q(xs, xr, xs_sem, xr_sem)
    send_a = to_q(xs, xra, xas_sem, xar_sem)
    send_b = to_q(bs, br, bs_sem, br_sem)

    def to_g(src, dst, send_sem, recv_sem):
        def one(p, dh, off):
            dest = peer(gy, off, NGY // 2)
            half = (h + dh) % NH
            return pltpu.make_async_remote_copy(
                src.at[p, half, dest], dst.at[p, h, gy],
                send_sem.at[p, dh, off], recv_sem.at[p, dh, off],
                device_id=(dest, half * NQ + q), device_id_type=MESH)
        return one

    send_g = to_g(gs, gr, gs_sem, gr_sem)
    send_ga = to_g(gsa, gra, gas_sem, gar_sem)

    def send_h(p, dh, off):
        dest = peer(gy, off, NGY // 2)
        return pltpu.make_async_remote_copy(
            hs.at[p, dest], hg.at[p, h, gy], hs_sem.at[p, dh, off], hr_sem.at[p, dh, off],
            device_id=(dest, (h + dh) % NH * NQ + q), device_id_type=MESH)

    def own_x(g):
        return pltpu.make_async_copy(xs.at[g, q], xr.at[g, q], loc_sem.at[g])

    def own_a(g):
        return pltpu.make_async_copy(xs.at[g, q], xra.at[g, q], loc_sem.at[4 + g])

    def own_b(g):
        return pltpu.make_async_copy(bs.at[g, q], br.at[g, q], loc_sem.at[8 + g])

    def own_g(p):
        return pltpu.make_async_copy(gs.at[p, h, gy], gr.at[p, h, gy], loc_sem.at[12 + p])

    def own_ga(p):
        return pltpu.make_async_copy(gsa.at[p, h, gy], gra.at[p, h, gy], loc_sem.at[14 + p])

    def own_h(p):
        return pltpu.make_async_copy(hs.at[p, gy], hg.at[p, h, gy], loc_sem.at[16 + p])

    def x_stage(g, field):
        for pair in range(C // 2):
            parts = []
            for j in range(2):
                rows = field(2 * pair + j, pl.ds(g * GY, GY)).reshape(GY * RZ, LEN)
                parts.append(dot_nt(ex[...], rows).reshape(NQ, NH * BA, GY * RZ))
            xs[g, :, pair * 16:(pair + 1) * 16, :] = jnp.concatenate(parts, axis=1).astype(BF)

    def field_x(c, ys):
        return v[c, ys]

    def field_a(c, ys):
        return (pit[c, ys].astype(F32) + mixing[c] * pres[c, ys].astype(F32)).astype(BF)

    def field_b(c, ys):
        return step[c, ys].astype(BF)

    def z_stage(g, src, dst):
        left = jnp.concatenate([src[g, s] for s in range(NQ)], axis=1)
        part = dot(left, kz[...]).reshape(C // 2, 2, 8, 512)
        halves = swap_rows(part[:, 0], part[:, 1])
        for half in range(NH):
            block = halves[half].reshape(HALF, 512)
            if g % 2 == 0:
                pf[half] = block
            else:
                for j in range(4):
                    cut = slice(j * 128, (j + 1) * 128)
                    even, odd = swap_lanes(pf[half, :, cut], block[:, cut])
                    dst[g // 2, half, 2 * j] = even.astype(BF)
                    dst[g // 2, half, 2 * j + 1] = odd.astype(BF)

    def y_stage(src):
        left = jnp.concatenate(
            [(src[p, 0, s].astype(F32) + src[p, 1, s].astype(F32)).astype(BF)
             for s in range(NGY) for p in range(2)], axis=1)
        return dot(left, ky[...])

    def mix_stage(sums):
        modes = sums.astype(BF).astype(F32).reshape(C // 2, 8, 512)
        for m in range(4):
            here = modes[:, :, m * 128:(m + 1) * 128]
            there = pltpu.roll(here, BA, 1)
            even, odd = swap_lanes(here, there)
            qm[2 * m * HALF:(2 * m + 1) * HALF, :] = even.reshape(HALF, 128)
            qm[(2 * m + 1) * HALF:(2 * m + 2) * HALF, :] = odd.reshape(HALF, 128)
        for a in range(BA):
            for t in range(C // 2):
                qt[a, t] = qm[pl.ds(t * 8 + a, BK, stride=HALF), :]

        def one(o, carry):
            for a in range(BA):
                total = jnp.zeros((BK, 128), F32)
                for t in range(C // 2):
                    total = total + wts[a, o, :, t * 128:(t + 1) * 128].astype(F32) * qt[a, t]
                row = pl.multiple_of((o * BA + a) * BK, BK)
                mo[pl.ds(row, BK), :] = total + pltpu.roll(total, 64, 1)
            return carry

        lax.fori_loop(0, C, one, 0)

    def yi_stage():
        low = iota((HALF, 128), 1) < 64
        left = jnp.concatenate(
            [jnp.where(low, mo[pl.ds(2 * m, HALF, stride=BK), :], mo[pl.ds(2 * m + 1, HALF, stride=BK), :])
             for m in range(4)], axis=1).astype(BF)
        for s in range(NGY):
            back = dot(left, kyi[:, s * 256:(s + 1) * 256]).astype(BF)
            hs[0, s] = back[:, :128]
            hs[1, s] = back[:, 128:]

    def zi_stage(p):
        cuts = {}
        for half in range(NH):
            for j in range(4):
                one = hg[p, half, 2 * j].astype(F32)
                two = hg[p, half, 2 * j + 1].astype(F32)
                cuts[half, j] = swap_lanes(one, two)
        for e in range(2):
            zero = jnp.concatenate([cuts[0, j][e] for j in range(4)], axis=1).reshape(C // 2, 8, 512)
            one = jnp.concatenate([cuts[1, j][e] for j in range(4)], axis=1).reshape(C // 2, 8, 512)
            even, odd = swap_rows(zero, one)
            left = jnp.concatenate([even, odd], axis=1).reshape(ROWS, 512).astype(BF)
            for s in range(0, NQ, 2):
                back = dot(left, kzi[:, s * 128:(s + 2) * 128]).astype(BF)
                bs[2 * p + e, s] = back[:, :128]
                bs[2 * p + e, s + 1] = back[:, 128:]

    def build_lhs():
        rows_o = iota((C * RZ, C), 0) // RZ
        pick = jnp.where(rows_o == iota((C * RZ, C), 1), 1.0, 0.0).astype(BF)
        col = iota((C, C * RZ), 1) // RZ
        spread = jnp.where(col == iota((C, C * RZ), 0), 1.0, 0.0).astype(BF)
        wide = dot(dot(pick, point_w[...]).astype(BF), spread)
        same = iota((C * RZ, C * RZ), 0) % RZ == iota((C * RZ, C * RZ), 1) % RZ
        wide = jnp.where(same, wide, 0.0)
        col3 = iota((3, 3 * RZ), 1) // RZ
        spread3 = jnp.where(col3 == iota((3, 3 * RZ), 0), 1.0, 0.0).astype(BF)
        lift = dot(dot_nt(pick, lift_w[...]).astype(BF), spread3)
        same3 = iota((C * RZ, 3 * RZ), 0) % RZ == iota((C * RZ, 3 * RZ), 1) % RZ
        lift = jnp.where(same3, lift, 0.0)
        bias = lift_b[...]
        hi = bias.astype(BF).astype(F32)
        mid = (bias - hi).astype(BF).astype(F32)
        lo = (bias - hi - mid).astype(BF).astype(F32)
        row = iota((16, C), 0)
        pieces = jnp.where(row == 0, hi, jnp.where(row == 1, mid, jnp.where(row == 2, lo, 0.0)))
        bias_cols = dot_nt(pick, pieces.astype(BF))
        full = jnp.concatenate([wide, lift, bias_cols], axis=1).astype(BF)
        for y in range(GY):
            lhs[y, :, 0:384] = full
        ones[...] = jnp.ones((16, LEN), BF)

    def turn_stage(g):
        for pair in range(C // 2):
            tile = br[g, :, pair * 16:(pair + 1) * 16, :].astype(F32)
            for j in range(2):
                block = tile[:, 8 * j:8 * j + 8].reshape(KM, GY * RZ)
                turned = jnp.transpose(block, (1, 0)).astype(BF).reshape(GY, RZ, KM)
                o = 2 * pair + j
                lhs[:, o * RZ:(o + 1) * RZ, 384:448] = turned

    def field_row(y):
        return v[:, y].reshape(C * RZ, LEN)

    def pre_activation(yl, y):
        right = jnp.concatenate(
            [field_row(y), forc[:, y].reshape(3 * RZ, LEN), ones[...], ix[...]], axis=0)
        osc[...] = dot(lhs[yl][:, :448], right)

    def final_first(g):
        turn_stage(g)

        def row(yl, carry):
            y = g * GY + yl
            pre_activation(yl, y)
            s_oo = jnp.zeros((RZ, LEN), F32)
            s_on = jnp.zeros((RZ, LEN), F32)
            s_nn = jnp.zeros((RZ, LEN), F32)
            for o in range(C):
                current = v[o, y].astype(F32)
                earlier = pres[o, y].astype(F32)
                newest = gelu(osc[o * RZ:(o + 1) * RZ, :]) - current
                step[o, y] = current + mixing[o] * newest
                s_oo += earlier * earlier
                s_on += earlier * newest
                s_nn += newest * newest
            acc[0] += s_oo
            acc[1] += s_on
            acc[2] += s_nn
            return carry

        lax.fori_loop(0, GY, row, 0)

    def final_second(g):
        turn_stage(g)

        def row(yl, carry):
            y = g * GY + yl
            pre_activation(yl, y)
            for o in range(C):
                current = v[o, y].astype(F32)
                pres[o, y] = (gelu(osc[o * RZ:(o + 1) * RZ, :]) - current).astype(BF)
            return carry

        lax.fori_loop(0, GY, row, 0)

    def combine(g, w_old, w_new):
        def one(c, carry):
            ys = pl.ds(g * GY, GY)
            old = pit[c, ys].astype(F32) + mixing[c] * pres[c, ys].astype(F32)
            v[c, ys] = (w_old * old + w_new * step[c, ys]).astype(BF)
            return carry

        lax.fori_loop(0, C, one, 0)

    def start_norms(kind):
        sends = []
        if kind == 0:
            rows = iota((8, 128), 0)
            mine = jnp.zeros((8, 128), F32)
            for n in range(3):
                total = jnp.sum(acc[n], axis=0, keepdims=True)
                mine = jnp.where(rows == n, total[:, :128] + total[:, 128:], mine)
            ar1[gz] = mine
            for off in range(1, 16):
                sends.append(pltpu.make_async_remote_copy(
                    ar1.at[gz], ar1.at[gz], s1_sem.at[off], r1_sem.at[off],
                    device_id=(gy, (gz + off) % 16), device_id_type=MESH))
        else:
            for off in range(1, 16):
                src = (gz - off + 16) % 16
                pltpu.make_async_remote_copy(
                    ar1.at[gz], ar1.at[src], s1_sem.at[off], r1_sem.at[off],
                    device_id=(gy, src), device_id_type=MESH).wait_recv()
            total = ar1[0]
            for s in range(1, 16):
                total = total + ar1[s]
            ar2[gy] = total
            for off in range(1, NGY):
                sends.append(pltpu.make_async_remote_copy(
                    ar2.at[gy], ar2.at[gy], s2_sem.at[off], r2_sem.at[off],
                    device_id=((gy + off) % NGY, gz), device_id_type=MESH))
        for copy in sends:
            copy.start()
        return sends

    def end_norms():
        for off in range(1, NGY):
            src = (gy - off + NGY) % NGY
            pltpu.make_async_remote_copy(
                ar2.at[gy], ar2.at[src], s2_sem.at[off], r2_sem.at[off],
                device_id=(src, gz), device_id_type=MESH).wait_recv()
        total = ar2[0]
        for s in range(1, NGY):
            total = total + ar2[s]
        sums = jnp.sum(total, axis=1, keepdims=True)
        norm_old, cross, norm_new = sums[0:1], sums[1:2], sums[2:3]
        ridge = REG * (norm_old + norm_new) + EPS
        denominator = norm_old + norm_new - 2.0 * cross + 2.0 * ridge
        w_old = (norm_new + ridge - cross) / denominator
        w_new = (norm_old + ridge - cross) / denominator
        weights_out[0] = w_old[0, 0]
        weights_out[1] = w_new[0, 0]
        return w_old, w_new

    def x_part(g):
        for off in range(1, NQ):
            send_x(g, off).start()
        own_x(g).start()

    def a_part(g):
        for off in range(1, NQ):
            send_x(g, off).wait_send()
        x_stage(g, field_a)
        for off in range(1, NQ):
            send_a(g, off).start()
        own_a(g).start()

    def b_part(g):
        for off in range(1, NQ):
            send_a(g, off).wait_send()
        x_stage(g, field_b)
        x_part(g)

    def z_part(g):
        own_x(g).wait()
        for off in range(1, NQ):
            send_x(g, off).wait_recv()
        z_stage(g, xr, gs)
        if g % 2 == 1:
            for dh, off in PEERS:
                send_g(g // 2, dh, off).start()
            own_g(g // 2).start()

    def za_part(g):
        own_a(g).wait()
        for off in range(1, NQ):
            send_a(g, off).wait_recv()
        z_stage(g, xra, gsa)
        if g % 2 == 1:
            for dh, off in PEERS:
                send_ga(g // 2, dh, off).start()
            own_ga(g // 2).start()

    def g_wait():
        for p in range(2):
            own_g(p).wait()
            for dh, off in PEERS:
                send_g(p, dh, off).wait_recv()

    def g_sent():
        for p in range(2):
            for dh, off in PEERS:
                send_g(p, dh, off).wait_send()

    def ga_wait():
        for p in range(2):
            own_ga(p).wait()
            for dh, off in PEERS:
                send_ga(p, dh, off).wait_recv()

    def h_part():
        yi_stage()
        for p in range(2):
            for dh, off in PEERS:
                send_h(p, dh, off).start()
            own_h(p).start()

    def zi_part(p):
        own_h(p).wait()
        for dh, off in PEERS:
            send_h(p, dh, off).wait_recv()
        zi_stage(p)
        for g in (2 * p, 2 * p + 1):
            for off in range(1, NQ):
                send_b(g, off).start()
            own_b(g).start()

    def b_wait(g):
        own_b(g).wait()
        for off in range(1, NQ):
            send_b(g, off).wait_recv()

    def inverse_sent():
        for p in range(2):
            for dh, off in PEERS:
                send_h(p, dh, off).wait_send()
        for g in range(GROUPS):
            for off in range(1, NQ):
                send_b(g, off).wait_send()

    for g in range(GROUPS):
        in_copies[g].wait()
        x_stage(g, field_x)
        if g == 0:
            pl.semaphore_wait(barrier, 29)
        x_part(g)
    acc[...] = jnp.zeros((3, RZ, LEN), F32)
    build_lhs()
    loads["kz"].wait()
    for g in range(GROUPS):
        z_part(g)
    loads["pres"].wait()
    loads["pit"].wait()
    a_part(0)
    a_part(1)
    for name in ("ky", "wts", "kyi", "kzi", "forc"):
        loads[name].wait()
    g_wait()
    mix_stage(y_stage(gr))
    h_part()
    a_part(2)
    a_part(3)
    zi_part(0)
    zi_part(1)
    g_sent()
    za_part(0)
    za_part(1)
    b_wait(0)
    final_first(0)
    b_part(0)
    za_part(2)
    za_part(3)
    for g in range(1, GROUPS):
        b_wait(g)
        final_first(g)
        b_part(g)
    sends = start_norms(0)
    inverse_sent()

    z_part(0)
    z_part(1)
    sends += start_norms(1)
    ga_wait()
    qa[...] = y_stage(gra)
    z_part(2)
    z_part(3)
    w_old, w_new = end_norms()
    g_wait()
    mix_stage(w_old * qa[...] + w_new * y_stage(gr))
    h_part()
    for g in range(GROUPS):
        combine(g, w_old.reshape(1, 1, 1), w_new.reshape(1, 1, 1))
    zi_part(0)
    zi_part(1)
    out_copies = []
    for g in range(GROUPS):
        b_wait(g)
        final_second(g)
        ys = pl.ds(g * GY, GY)
        out_copies.append(pltpu.make_async_copy(pres.at[:, ys], out.at[:, ys], out_sem.at[g]))
        out_copies[-1].start()
    for copy in sends:
        copy.wait_send()
    for g in range(GROUPS):
        for off in range(1, NQ):
            send_x(g, off).wait_send()
    g_sent()
    for p in range(2):
        for dh, off in PEERS:
            send_ga(p, dh, off).wait_send()
    inverse_sent()
    for copy in out_copies:
        copy.wait()


def shards(forcing, lift_weight, lift_bias, point_weight, spectral_weight, mixing, iterate, prev_iterate, prev_residual):
    ex, ix, kz, kzi, ky, kyi = (jnp.asarray(t) for t in tables())
    field = (C, RY, RZ, LEN)
    vmem = pl.BlockSpec(memory_space=pltpu.VMEM)
    smem = pl.BlockSpec(memory_space=pltpu.SMEM)
    hbm = pl.BlockSpec(memory_space=pl.ANY)
    dma = pltpu.SemaphoreType.DMA
    scratch = [
        pltpu.VMEM(field, BF),
        pltpu.VMEM(field, BF),
        pltpu.VMEM(field, BF),
        pltpu.VMEM(field, F32),
        pltpu.VMEM((3, RY, RZ, LEN), BF),
        pltpu.VMEM((BA, C, BK, C * KM), BF),
        pltpu.VMEM((GY, C * RZ, 512), BF),
        pltpu.VMEM((GROUPS, NQ, ROWS, 128), BF),
        pltpu.VMEM((GROUPS, NQ, ROWS, 128), BF),
        pltpu.VMEM((GROUPS, NQ, ROWS, 128), BF),
        pltpu.VMEM((GROUPS, NQ, ROWS, 128), BF),
        pltpu.VMEM((GROUPS, NQ, ROWS, 128), BF),
        pltpu.VMEM((NH, HALF, 512), F32),
        pltpu.VMEM((2, NH, NGY, HALF, 128), BF),
        pltpu.VMEM((2, NH, NGY, HALF, 128), BF),
        pltpu.VMEM((2, NH, NGY, HALF, 128), BF),
        pltpu.VMEM((2, NH, NGY, HALF, 128), BF),
        pltpu.VMEM((2, NGY, HALF, 128), BF),
        pltpu.VMEM((2, NH, NGY, HALF, 128), BF),
        pltpu.VMEM((1024, 512), BF),
        pltpu.VMEM((512, 1024), BF),
        pltpu.VMEM((2048, 512), BF),
        pltpu.VMEM((512, 2048), BF),
        pltpu.VMEM((BK * HALF, 128), F32),
        pltpu.VMEM((BA, C // 2, BK, 128), F32),
        pltpu.VMEM((HALF, 512), F32),
        pltpu.VMEM((BK * HALF, 128), F32),
        pltpu.VMEM((C * RZ, LEN), F32),
        pltpu.VMEM((3, RZ, LEN), F32),
        pltpu.VMEM((16, 8, 128), F32),
        pltpu.VMEM((NGY, 8, 128), F32),
        pltpu.VMEM((16, LEN), BF),
        dma((8,)), dma((GROUPS,)), dma((GROUPS,)), dma((18,)),
        dma((GROUPS, NQ)), dma((GROUPS, NQ)), dma((GROUPS, NQ)), dma((GROUPS, NQ)),
        dma((GROUPS, NQ)), dma((GROUPS, NQ)),
        dma((2, NH, NGY)), dma((2, NH, NGY)), dma((2, NH, NGY)), dma((2, NH, NGY)),
        dma((2, NH, NGY)), dma((2, NH, NGY)),
        dma((16,)), dma((16,)), dma((NGY,)), dma((NGY,)),
    ]
    result, weights = pl.pallas_call(
        kernel,
        out_shape=(
            jax.ShapeDtypeStruct(field, BF),
            jax.ShapeDtypeStruct((2,), F32),
        ),
        in_specs=[hbm, vmem, vmem, vmem, hbm, smem, hbm, hbm, hbm, vmem, vmem, hbm, hbm, hbm, hbm],
        out_specs=(hbm, smem),
        scratch_shapes=scratch,
        compiler_params=pltpu.CompilerParams(
            collective_id=0, has_side_effects=True, vmem_limit_bytes=60 * 1024 * 1024),
        cost_estimate=pl.CostEstimate(
            flops=10_000_000_000, bytes_accessed=40_000_000, transcendentals=5_000_000),
    )(forcing, lift_weight.T, lift_bias.reshape(1, C), point_weight,
      jnp.transpose(spectral_weight, (0, 2, 1, 3)), mixing,
      iterate, prev_iterate, prev_residual, ex, ix, kz, kzi, ky, kyi)
    return result, weights


def solution(mesh):
    in_specs = (
        P(None, "gy", "gz", None),
        P(),
        P(),
        P(),
        P("gz", "gy", None, None),
        P(),
        P(None, "gy", "gz", None),
        P(None, "gy", "gz", None),
        P(None, "gy", "gz", None),
    )
    out_specs = (P(None, "gy", "gz", None), P())
    return jax.shard_map(shards, mesh=mesh, in_specs=in_specs, out_specs=out_specs, check_vma=False)
```

```python
import functools
import math

import jax
import jax.numpy as jnp
import ml_dtypes
import numpy as np
from jax import lax
from jax.experimental import pallas as pl
from jax.experimental.pallas import tpu as pltpu
from jax.sharding import PartitionSpec as P

MESH = pl.DeviceIdType.MESH
BF = jnp.bfloat16
F32 = jnp.float32

MODES = 32
KM = 64
REG = 0.001
EPS = 1e-06

C = 20
LEN = 256
NGY = 8
NQ = 8
NH = 2
RY = 32
RZ = 16
GROUPS = 4
GY = 8
BA = 4
BK = 8
ROWS = C * NH * BA
HALF = C * BA


WIDE = 48


def ring_steps(off, ring):
    return min(off // 2, ring - off // 2)


PEERS = sorted(
    [(dh, off) for off in range(NGY) for dh in range(NH) if (dh, off) != (0, 0)],
    key=lambda t: -(ring_steps(t[1], NGY // 2) + (1 if t[1] % 2 else 2 * t[0])))
QPEERS = sorted(range(1, NQ), key=lambda t: -ring_steps(t, NQ // 2))


def dft_table(length):
    positions = np.arange(length)[:, None]
    waves = np.arange(2 * MODES)[None, :]
    number = np.where(waves < MODES, waves, waves - MODES + 1)
    angles = (positions * number % length).astype(np.float32) * np.float32(2.0 * math.pi / length)
    both = np.where(waves < MODES, np.cos(angles), np.sin(angles)).astype(np.float32)
    inverse = (both * np.float32(2.0 / length)).astype(ml_dtypes.bfloat16)
    return both.astype(ml_dtypes.bfloat16), inverse


@functools.lru_cache(maxsize=None)
def tables():
    fwd, inv = dft_table(LEN)
    f = fwd.astype(np.float32)
    i = inv.astype(np.float32)
    order = np.arange(KM).reshape(NH, NQ, BA).transpose(1, 0, 2).reshape(-1)
    ex = f[:, order].T
    ix = i[:, order].T
    eye_y = np.eye(GY, dtype=np.float32)
    eye_k = np.eye(BK, dtype=np.float32)
    kz = np.einsum("hqzgk,yw->hqyzgwk", f.reshape(NH, NQ, RZ, NGY, BK), eye_y)
    kz = kz.reshape(NH, NQ * GY * RZ, NGY * GY * BK)
    kzi = np.einsum("hqzgk,yw->hgykqwz", i.reshape(NH, NQ, RZ, NGY, BK), eye_y)
    kzi = kzi.reshape(NH, NGY * GY * BK, NQ * GY * RZ)
    ky = np.einsum("yb,kj->ykjb", f, eye_k).reshape(LEN * BK, BK * KM)
    kyi = np.einsum("yb,kj->kbyj", i, eye_k).reshape(BK * KM, LEN * BK)
    return tuple(np.ascontiguousarray(t).astype(ml_dtypes.bfloat16) for t in (ex, ix, kz, kzi, ky, kyi))


def iota(shape, axis):
    return lax.broadcasted_iota(jnp.int32, shape, axis)


def dot(a, b):
    return jnp.dot(a, b, preferred_element_type=F32)


def dot_nt(a, b):
    return lax.dot_general(a, b, (((1,), (1,)), ((), ())), preferred_element_type=F32)


def peer(place, off, ring):
    return (place // 2 + off // 2) % ring * 2 + (place + off) % 2


def swap_rows(first, second):
    low = iota(first.shape, 1) < BA
    return (
        jnp.where(low, first, pltpu.roll(second, BA, 1)),
        jnp.where(low, pltpu.roll(first, BA, 1), second),
    )


def swap_lanes(first, second):
    axis = first.ndim - 1
    low = iota(first.shape, axis) < 64
    return (
        jnp.where(low, first, pltpu.roll(second, 64, axis)),
        jnp.where(low, pltpu.roll(first, 64, axis), second),
    )


def gelu(x):
    inner = x * (math.sqrt(2.0 / math.pi) + (math.sqrt(2.0 / math.pi) * 0.044715) * (x * x))
    half = 0.5 * x
    return half + half * jnp.tanh(inner)


def kernel(
    forcing, lift_w, lift_b, point_w, spec_w, mixing, iterate, prev_it, prev_res,
    ex, ix, kz_all, kzi_all, ky_hbm, kyi_hbm,
    out, weights_out,
    v, pit, pres, step, forc, wts, lhs, xs, xr, xsa, xra, bs, br, gs, gr, gsa, gra, hs, hg,
    kz, kzi, ky, kyi, qm, qt, qa, mo, osc0, osc1, acc, ar1, ar2, ones,
    load_sem, in_sem, out_sem, loc_sem,
    xs_sem, xr_sem, xas_sem, xar_sem, bs_sem, br_sem, gs_sem, gr_sem, gas_sem, gar_sem, hs_sem, hr_sem,
    s1_sem, r1_sem, s2_sem, r2_sem,
):
    gy = lax.axis_index("gy")
    gz = lax.axis_index("gz")
    h = gz // NQ
    q = gz % NQ
    q_to = {off: peer(q, off, NQ // 2) for off in QPEERS}
    q_gz = {off: h * NQ + q_to[off] for off in QPEERS}
    y_to = {off: peer(gy, off, NGY // 2) for off in range(NGY)}
    h_to = [h, 1 - h]
    h_gz = [gz, (1 - h) * NQ + q]

    barrier = pltpu.get_barrier_semaphore()
    for dh, off in PEERS:
        pl.semaphore_signal(barrier, inc=1, device_id=(y_to[off], h_gz[dh]), device_id_type=MESH)
    for off in QPEERS:
        pl.semaphore_signal(barrier, inc=1, device_id=(gy, q_gz[off]), device_id_type=MESH)

    in_copies = [
        pltpu.make_async_copy(
            iterate.at[:, pl.ds(g * GY, GY)], v.at[:, pl.ds(g * GY, GY)], in_sem.at[g]
        )
        for g in range(GROUPS)
    ]
    loads = {
        name: pltpu.make_async_copy(src, dst, load_sem.at[n])
        for n, (name, src, dst) in enumerate([
            ("kz", kz_all.at[h], kz),
            ("pres", prev_res, pres),
            ("pit", prev_it, pit),
            ("ky", ky_hbm, ky),
            ("wts", spec_w, wts),
            ("kyi", kyi_hbm, kyi),
            ("kzi", kzi_all.at[h], kzi),
            ("forc", forcing, forc),
        ])
    }
    for copy in in_copies:
        copy.start()

    def to_q(src, dst, send_sem, recv_sem):
        def one(g, off):
            return pltpu.make_async_remote_copy(
                src.at[g, q_to[off]], dst.at[g, q], send_sem.at[g, off], recv_sem.at[g, off],
                device_id=(gy, q_gz[off]), device_id_type=MESH)
        return one

    send_x = to_q(xs, xr, xs_sem, xr_sem)
    send_a = to_q(xsa, xra, xas_sem, xar_sem)
    send_b = to_q(bs, br, bs_sem, br_sem)

    def to_g(src, dst, send_sem, recv_sem):
        def one(p, dh, off):
            return pltpu.make_async_remote_copy(
                src.at[p, h_to[dh], y_to[off]], dst.at[p, h, gy],
                send_sem.at[p, dh, off], recv_sem.at[p, dh, off],
                device_id=(y_to[off], h_gz[dh]), device_id_type=MESH)
        return one

    send_g = to_g(gs, gr, gs_sem, gr_sem)
    send_ga = to_g(gsa, gra, gas_sem, gar_sem)

    def send_h(p, dh, off):
        return pltpu.make_async_remote_copy(
            hs.at[p, y_to[off]], hg.at[p, h, gy], hs_sem.at[p, dh, off], hr_sem.at[p, dh, off],
            device_id=(y_to[off], h_gz[dh]), device_id_type=MESH)

    def own_x(g):
        return pltpu.make_async_copy(xs.at[g, q], xr.at[g, q], loc_sem.at[g])

    def own_a(g):
        return pltpu.make_async_copy(xsa.at[g, q], xra.at[g, q], loc_sem.at[4 + g])

    def own_b(g):
        return pltpu.make_async_copy(bs.at[g, q], br.at[g, q], loc_sem.at[8 + g])

    def own_g(p):
        return pltpu.make_async_copy(gs.at[p, h, gy], gr.at[p, h, gy], loc_sem.at[12 + p])

    def own_ga(p):
        return pltpu.make_async_copy(gsa.at[p, h, gy], gra.at[p, h, gy], loc_sem.at[16 + p])

    def own_h(p):
        return pltpu.make_async_copy(hs.at[p, gy], hg.at[p, h, gy], loc_sem.at[20 + p])

    def x_stage(g, field, dst):
        for pair in range(C // 2):
            parts = []
            for j in range(2):
                rows = field(2 * pair + j, pl.ds(g * GY, GY)).reshape(GY * RZ, LEN)
                parts.append(dot_nt(ex[...], rows).reshape(NQ, NH * BA, GY * RZ))
            dst[g, :, pair * 16:(pair + 1) * 16, :] = jnp.concatenate(parts, axis=1).astype(BF)

    def field_x(c, ys):
        return v[c, ys]

    def field_a(c, ys):
        return (pit[c, ys].astype(F32) + mixing[c] * pres[c, ys].astype(F32)).astype(BF)

    def field_b(c, ys):
        return step[c, ys].astype(BF)

    def z_stage(g, src, dst):
        left = jnp.concatenate([src[g, s] for s in range(NQ)], axis=1)
        part = dot(left, kz[...]).reshape(C // 2, 2, 8, 512)
        halves = swap_rows(part[:, 0], part[:, 1])
        for half in range(NH):
            block = halves[half].reshape(HALF, 512)
            for j in range(4):
                cut = block[:, j * 128:(j + 1) * 128]
                even, odd = swap_lanes(cut[:WIDE], cut[HALF - WIDE:])
                dst[g, half, 2 * j] = even.astype(BF)
                dst[g, half, 2 * j + 1] = odd.astype(BF)

    def unfold(first, second):
        top, bottom = swap_lanes(first, second)
        return jnp.concatenate([top, bottom[2 * WIDE - HALF:]], axis=0)

    def y_stage(src):
        parts = []
        for s in range(NGY):
            for p in range(2):
                pair = [src[g, 0, s].astype(F32) + src[g, 1, s].astype(F32) for g in (2 * p, 2 * p + 1)]
                parts.append(unfold(*pair).astype(BF))
        return dot(jnp.concatenate(parts, axis=1), ky[...])

    def mix_stage(sums):
        modes = sums.astype(BF).astype(F32).reshape(C // 2, 8, 512)
        for m in range(4):
            here = modes[:, :, m * 128:(m + 1) * 128]
            there = pltpu.roll(here, BA, 1)
            even, odd = swap_lanes(here, there)
            qm[2 * m * HALF:(2 * m + 1) * HALF, :] = even.reshape(HALF, 128)
            qm[(2 * m + 1) * HALF:(2 * m + 2) * HALF, :] = odd.reshape(HALF, 128)
        for a in range(BA):
            for t in range(C // 2):
                qt[a, t] = qm[pl.ds(t * 8 + a, BK, stride=HALF), :]

        def one(o, carry):
            for a in range(BA):
                total = jnp.zeros((BK, 128), F32)
                for t in range(C // 2):
                    total = total + wts[a, o, :, t * 128:(t + 1) * 128].astype(F32) * qt[a, t]
                row = pl.multiple_of((o * BA + a) * BK, BK)
                mo[pl.ds(row, BK), :] = total + pltpu.roll(total, 64, 1)
            return carry

        lax.fori_loop(0, C, one, 0, unroll=4)

    def yi_stage():
        low = iota((HALF, 128), 1) < 64
        left = jnp.concatenate(
            [jnp.where(low, mo[pl.ds(2 * m, HALF, stride=BK), :], mo[pl.ds(2 * m + 1, HALF, stride=BK), :])
             for m in range(4)], axis=1).astype(BF)
        for s in range(NGY):
            back = dot(left, kyi[:, s * 256:(s + 1) * 256])
            for p in range(2):
                cut = back[:, p * 128:(p + 1) * 128]
                even, odd = swap_lanes(cut[:WIDE], cut[HALF - WIDE:])
                hs[2 * p, s] = even.astype(BF)
                hs[2 * p + 1, s] = odd.astype(BF)

    def zi_stage(g):
        halves = [
            jnp.concatenate(
                [unfold(hg[g, half, 2 * j].astype(F32), hg[g, half, 2 * j + 1].astype(F32)) for j in range(4)],
                axis=1).reshape(C // 2, 8, 512)
            for half in range(NH)
        ]
        even, odd = swap_rows(*halves)
        left = jnp.concatenate([even, odd], axis=1).reshape(ROWS, 512).astype(BF)
        for s in range(0, NQ, 2):
            back = dot(left, kzi[:, s * 128:(s + 2) * 128]).astype(BF)
            bs[g, s] = back[:, :128]
            bs[g, s + 1] = back[:, 128:]

    def build_lhs():
        rows_o = iota((C * RZ, C), 0) // RZ
        pick = jnp.where(rows_o == iota((C * RZ, C), 1), 1.0, 0.0).astype(BF)
        col = iota((C, C * RZ), 1) // RZ
        spread = jnp.where(col == iota((C, C * RZ), 0), 1.0, 0.0).astype(BF)
        wide = dot(dot(pick, point_w[...]).astype(BF), spread)
        same = iota((C * RZ, C * RZ), 0) % RZ == iota((C * RZ, C * RZ), 1) % RZ
        wide = jnp.where(same, wide, 0.0)
        col3 = iota((3, 3 * RZ), 1) // RZ
        spread3 = jnp.where(col3 == iota((3, 3 * RZ), 0), 1.0, 0.0).astype(BF)
        lift = dot(dot_nt(pick, lift_w[...]).astype(BF), spread3)
        same3 = iota((C * RZ, 3 * RZ), 0) % RZ == iota((C * RZ, 3 * RZ), 1) % RZ
        lift = jnp.where(same3, lift, 0.0)
        bias = lift_b[...]
        hi = bias.astype(BF).astype(F32)
        mid = (bias - hi).astype(BF).astype(F32)
        lo = (bias - hi - mid).astype(BF).astype(F32)
        row = iota((16, C), 0)
        pieces = jnp.where(row == 0, hi, jnp.where(row == 1, mid, jnp.where(row == 2, lo, 0.0)))
        bias_cols = dot_nt(pick, pieces.astype(BF))
        full = jnp.concatenate([wide, lift, bias_cols], axis=1).astype(BF)
        for y in range(GY):
            lhs[y, :, 0:384] = full
        ones[...] = jnp.ones((16, LEN), BF)

    def turn_stage(g):
        for pair in range(C // 2):
            tile = br[g, :, pair * 16:(pair + 1) * 16, :].astype(F32)
            for j in range(2):
                block = tile[:, 8 * j:8 * j + 8].reshape(KM, GY * RZ)
                turned = jnp.transpose(block, (1, 0)).astype(BF).reshape(GY, RZ, KM)
                o = 2 * pair + j
                lhs[:, o * RZ:(o + 1) * RZ, 384:448] = turned

    def field_row(y):
        return v[:, y].reshape(C * RZ, LEN)

    def pre_activation(yl, y, dst):
        right = jnp.concatenate(
            [field_row(y), forc[:, y].reshape(3 * RZ, LEN), ones[...], ix[...]], axis=0)
        dst[...] = dot(lhs[yl][:, :448], right)

    def row_first(y, src):
        s_oo = jnp.zeros((RZ, LEN), F32)
        s_on = jnp.zeros((RZ, LEN), F32)
        s_nn = jnp.zeros((RZ, LEN), F32)
        for o in range(C):
            current = v[o, y].astype(F32)
            earlier = pres[o, y].astype(F32)
            newest = gelu(src[o * RZ:(o + 1) * RZ, :]) - current
            step[o, y] = current + mixing[o] * newest
            s_oo += earlier * earlier
            s_on += earlier * newest
            s_nn += newest * newest
        acc[0] += s_oo
        acc[1] += s_on
        acc[2] += s_nn

    def row_second(y, src):
        for o in range(C):
            current = v[o, y].astype(F32)
            pres[o, y] = (gelu(src[o * RZ:(o + 1) * RZ, :]) - current).astype(BF)

    def final(g, row):
        turn_stage(g)
        pre_activation(0, g * GY, osc0)

        def two_rows(i, carry):
            yl = 2 * i
            y = g * GY + yl
            pre_activation(yl + 1, y + 1, osc1)
            row(y, osc0)
            later = (yl + 2) % GY
            pre_activation(later, g * GY + later, osc0)
            row(y + 1, osc1)
            return carry

        lax.fori_loop(0, GY // 2, two_rows, 0)

    def combine(g, w_old, w_new):
        def one(c, carry):
            ys = pl.ds(g * GY, GY)
            old = pit[c, ys].astype(F32) + mixing[c] * pres[c, ys].astype(F32)
            v[c, ys] = (w_old * old + w_new * step[c, ys]).astype(BF)
            return carry

        lax.fori_loop(0, C, one, 0)

    def send_n1(off):
        return pltpu.make_async_remote_copy(
            ar1.at[q], ar1.at[q], s1_sem.at[off], r1_sem.at[off],
            device_id=(gy, q_gz[off]), device_id_type=MESH)

    def send_n2(dh, off):
        return pltpu.make_async_remote_copy(
            ar2.at[h, gy], ar2.at[h, gy], s2_sem.at[dh, off], r2_sem.at[dh, off],
            device_id=(y_to[off], h_gz[dh]), device_id_type=MESH)

    def start_norms():
        rows = iota((8, 128), 0)
        mine = jnp.zeros((8, 128), F32)
        for n in range(3):
            total = jnp.sum(acc[n], axis=0, keepdims=True)
            mine = jnp.where(rows == n, total[:, :128] + total[:, 128:], mine)
        ar1[q] = mine
        for off in QPEERS:
            send_n1(off).start()

    def next_norms():
        for off in QPEERS:
            send_n1(off).wait_recv()
        total = ar1[0]
        for s in range(1, NQ):
            total = total + ar1[s]
        ar2[h, gy] = total
        for dh, off in PEERS:
            send_n2(dh, off).start()

    def end_norms():
        for dh, off in PEERS:
            send_n2(dh, off).wait_recv()
        total = jnp.zeros((8, 128), F32)
        for half in range(NH):
            for s in range(NGY):
                total = total + ar2[half, s]
        sums = jnp.sum(total, axis=1, keepdims=True)
        norm_old, cross, norm_new = sums[0:1], sums[1:2], sums[2:3]
        ridge = REG * (norm_old + norm_new) + EPS
        denominator = norm_old + norm_new - 2.0 * cross + 2.0 * ridge
        w_old = (norm_new + ridge - cross) / denominator
        w_new = (norm_old + ridge - cross) / denominator
        weights_out[0] = w_old[0, 0]
        weights_out[1] = w_new[0, 0]
        return w_old, w_new

    def x_part(g):
        for off in QPEERS:
            send_x(g, off).start()
        own_x(g).start()

    def a_send(g):
        for off in QPEERS:
            send_a(g, off).start()
        own_a(g).start()

    def b_part(g):
        for off in QPEERS:
            send_x(g, off).wait_send()
        x_stage(g, field_b, xs)
        x_part(g)

    def z_part(g):
        own_x(g).wait()
        for off in QPEERS:
            send_x(g, off).wait_recv()
        z_stage(g, xr, gs)
        for dh, off in PEERS:
            send_g(g, dh, off).start()
        own_g(g).start()

    def za_part(g):
        own_a(g).wait()
        for off in QPEERS:
            send_a(g, off).wait_recv()
        z_stage(g, xra, gsa)
        for dh, off in PEERS:
            send_ga(g, dh, off).start()
        own_ga(g).start()

    def g_wait():
        for p in range(GROUPS):
            own_g(p).wait()
            for dh, off in PEERS:
                send_g(p, dh, off).wait_recv()

    def g_sent():
        for p in range(GROUPS):
            for dh, off in PEERS:
                send_g(p, dh, off).wait_send()

    def ga_wait():
        for p in range(GROUPS):
            own_ga(p).wait()
            for dh, off in PEERS:
                send_ga(p, dh, off).wait_recv()

    def h_part():
        yi_stage()
        h_send(0)
        h_send(1)

    def h_send(p):
        for dh, off in PEERS:
            send_h(p, dh, off).start()
        own_h(p).start()

    def zi_part(p):
        own_h(p).wait()
        for dh, off in PEERS:
            send_h(p, dh, off).wait_recv()
        zi_stage(p)
        for off in QPEERS:
            send_b(p, off).start()
        own_b(p).start()

    def b_wait(g):
        own_b(g).wait()
        for off in QPEERS:
            send_b(g, off).wait_recv()

    def inverse_sent():
        for p in range(GROUPS):
            for dh, off in PEERS:
                send_h(p, dh, off).wait_send()
        for g in range(GROUPS):
            for off in QPEERS:
                send_b(g, off).wait_send()

    for g in range(GROUPS):
        in_copies[g].wait()
        if g == 2:
            loads["kz"].start()
        x_stage(g, field_x, xs)
        if g == 0:
            pl.semaphore_wait(barrier, len(PEERS) + len(QPEERS))
        x_part(g)
    for name, copy in loads.items():
        if name != "kz":
            copy.start()
    acc[...] = jnp.zeros((3, RZ, LEN), F32)
    build_lhs()
    loads["kz"].wait()
    z_part(0)
    loads["pres"].wait()
    loads["pit"].wait()
    for g in range(1, GROUPS):
        x_stage(g - 1, field_a, xsa)
        z_part(g)
    for g in range(GROUPS - 1):
        a_send(g)
    x_stage(GROUPS - 1, field_a, xsa)
    a_send(GROUPS - 1)
    for name in ("ky", "wts", "kyi", "kzi", "forc"):
        loads[name].wait()
    g_wait()
    mix_stage(y_stage(gr))
    h_part()
    h_send(2)
    h_send(3)
    for g in range(GROUPS):
        zi_part(g)
    g_sent()
    za_part(0)
    za_part(1)
    b_wait(0)
    final(0, row_first)
    b_part(0)
    za_part(2)
    za_part(3)
    for g in range(1, GROUPS):
        b_wait(g)
        final(g, row_first)
        b_part(g)
    start_norms()
    inverse_sent()

    z_part(0)
    z_part(1)
    next_norms()
    ga_wait()
    qa[...] = y_stage(gra)
    z_part(2)
    z_part(3)
    w_old, w_new = end_norms()
    g_wait()
    mix_stage(w_old * qa[...] + w_new * y_stage(gr))
    h_part()
    parts = (w_old.reshape(1, 1, 1), w_new.reshape(1, 1, 1))
    combine(0, *parts)
    h_send(2)
    combine(1, *parts)
    h_send(3)
    for g in range(GROUPS):
        zi_part(g)
    combine(2, *parts)
    combine(3, *parts)
    out_copies = []
    for g in range(GROUPS):
        b_wait(g)
        final(g, row_second)
        ys = pl.ds(g * GY, GY)
        out_copies.append(pltpu.make_async_copy(pres.at[:, ys], out.at[:, ys], out_sem.at[g]))
        out_copies[-1].start()
    for off in QPEERS:
        send_n1(off).wait_send()
    for dh, off in PEERS:
        send_n2(dh, off).wait_send()
    for g in range(GROUPS):
        for off in QPEERS:
            send_x(g, off).wait_send()
            send_a(g, off).wait_send()
    g_sent()
    for p in range(GROUPS):
        for dh, off in PEERS:
            send_ga(p, dh, off).wait_send()
    inverse_sent()
    for copy in out_copies:
        copy.wait()


def shards(forcing, lift_weight, lift_bias, point_weight, spectral_weight, mixing, iterate, prev_iterate, prev_residual):
    ex, ix, kz, kzi, ky, kyi = (jnp.asarray(t) for t in tables())
    field = (C, RY, RZ, LEN)
    vmem = pl.BlockSpec(memory_space=pltpu.VMEM)
    smem = pl.BlockSpec(memory_space=pltpu.SMEM)
    hbm = pl.BlockSpec(memory_space=pl.ANY)
    dma = pltpu.SemaphoreType.DMA
    scratch = [
        pltpu.VMEM(field, BF),
        pltpu.VMEM(field, BF),
        pltpu.VMEM(field, BF),
        pltpu.VMEM(field, F32),
        pltpu.VMEM((3, RY, RZ, LEN), BF),
        pltpu.VMEM((BA, C, BK, C * KM), BF),
        pltpu.VMEM((GY, C * RZ, 512), BF),
        pltpu.VMEM((GROUPS, NQ, ROWS, 128), BF),
        pltpu.VMEM((GROUPS, NQ, ROWS, 128), BF),
        pltpu.VMEM((GROUPS, NQ, ROWS, 128), BF),
        pltpu.VMEM((GROUPS, NQ, ROWS, 128), BF),
        pltpu.VMEM((GROUPS, NQ, ROWS, 128), BF),
        pltpu.VMEM((GROUPS, NQ, ROWS, 128), BF),
        pltpu.VMEM((GROUPS, NH, NGY, WIDE, 128), BF),
        pltpu.VMEM((GROUPS, NH, NGY, WIDE, 128), BF),
        pltpu.VMEM((GROUPS, NH, NGY, WIDE, 128), BF),
        pltpu.VMEM((GROUPS, NH, NGY, WIDE, 128), BF),
        pltpu.VMEM((GROUPS, NGY, WIDE, 128), BF),
        pltpu.VMEM((GROUPS, NH, NGY, WIDE, 128), BF),
        pltpu.VMEM((1024, 512), BF),
        pltpu.VMEM((512, 1024), BF),
        pltpu.VMEM((2048, 512), BF),
        pltpu.VMEM((512, 2048), BF),
        pltpu.VMEM((BK * HALF, 128), F32),
        pltpu.VMEM((BA, C // 2, BK, 128), F32),
        pltpu.VMEM((HALF, 512), F32),
        pltpu.VMEM((BK * HALF, 128), F32),
        pltpu.VMEM((C * RZ, LEN), F32),
        pltpu.VMEM((C * RZ, LEN), F32),
        pltpu.VMEM((3, RZ, LEN), F32),
        pltpu.VMEM((NQ, 8, 128), F32),
        pltpu.VMEM((NH, NGY, 8, 128), F32),
        pltpu.VMEM((16, LEN), BF),
        dma((8,)), dma((GROUPS,)), dma((GROUPS,)), dma((24,)),
        dma((GROUPS, NQ)), dma((GROUPS, NQ)), dma((GROUPS, NQ)), dma((GROUPS, NQ)),
        dma((GROUPS, NQ)), dma((GROUPS, NQ)),
        dma((GROUPS, NH, NGY)), dma((GROUPS, NH, NGY)), dma((GROUPS, NH, NGY)), dma((GROUPS, NH, NGY)),
        dma((GROUPS, NH, NGY)), dma((GROUPS, NH, NGY)),
        dma((NQ,)), dma((NQ,)), dma((NH, NGY)), dma((NH, NGY)),
    ]
    result, weights = pl.pallas_call(
        kernel,
        out_shape=(
            jax.ShapeDtypeStruct(field, BF),
            jax.ShapeDtypeStruct((2,), F32),
        ),
        in_specs=[hbm, vmem, vmem, vmem, hbm, smem, hbm, hbm, hbm, vmem, vmem, hbm, hbm, hbm, hbm],
        out_specs=(hbm, smem),
        scratch_shapes=scratch,
        compiler_params=pltpu.CompilerParams(
            collective_id=0, has_side_effects=True, vmem_limit_bytes=60 * 1024 * 1024),
        cost_estimate=pl.CostEstimate(
            flops=10_000_000_000, bytes_accessed=40_000_000, transcendentals=5_000_000),
    )(forcing, lift_weight.T, lift_bias.reshape(1, C), point_weight,
      jnp.transpose(spectral_weight, (0, 2, 1, 3)), mixing,
      iterate, prev_iterate, prev_residual, ex, ix, kz, kzi, ky, kyi)
    return result, weights


def solution(mesh):
    in_specs = (
        P(None, "gy", "gz", None),
        P(),
        P(),
        P(),
        P("gz", "gy", None, None),
        P(),
        P(None, "gy", "gz", None),
        P(None, "gy", "gz", None),
        P(None, "gy", "gz", None),
    )
    out_specs = (P(None, "gy", "gz", None), P())
    return jax.shard_map(shards, mesh=mesh, in_specs=in_specs, out_specs=out_specs, check_vma=False)
```

```python
import functools
import math

import jax
import jax.numpy as jnp
import ml_dtypes
import numpy as np
from jax import lax
from jax.experimental import pallas as pl
from jax.experimental.pallas import tpu as pltpu
from jax.sharding import PartitionSpec as P

MESH = pl.DeviceIdType.MESH
BF = jnp.bfloat16
F32 = jnp.float32

MODES = 32
KM = 64
REG = 0.001
EPS = 1e-06

C = 20
LEN = 256
NGY = 8
NQ = 8
NH = 2
RY = 32
RZ = 16
GROUPS = 4
GY = 8
BA = 4
BK = 8
ROWS = C * NH * BA
HALF = C * BA


WIDE = 48


def ring_steps(off, ring):
    return min(off // 2, ring - off // 2)


PEERS = sorted(
    [(dh, off) for off in range(NGY) for dh in range(NH) if (dh, off) != (0, 0)],
    key=lambda t: -(ring_steps(t[1], NGY // 2) + (1 if t[1] % 2 else 2 * t[0])))
QPEERS = sorted(range(1, NQ), key=lambda t: -ring_steps(t, NQ // 2))


def dft_table(length):
    positions = np.arange(length)[:, None]
    waves = np.arange(2 * MODES)[None, :]
    number = np.where(waves < MODES, waves, waves - MODES + 1)
    angles = (positions * number % length).astype(np.float32) * np.float32(2.0 * math.pi / length)
    both = np.where(waves < MODES, np.cos(angles), np.sin(angles)).astype(np.float32)
    inverse = (both * np.float32(2.0 / length)).astype(ml_dtypes.bfloat16)
    return both.astype(ml_dtypes.bfloat16), inverse


@functools.lru_cache(maxsize=None)
def tables():
    fwd, inv = dft_table(LEN)
    f = fwd.astype(np.float32)
    i = inv.astype(np.float32)
    order = np.arange(KM).reshape(NH, NQ, BA).transpose(1, 0, 2).reshape(-1)
    ex = f[:, order].T
    ix = i[:, order].T
    eye_y = np.eye(GY, dtype=np.float32)
    eye_k = np.eye(BK, dtype=np.float32)
    kz = np.einsum("hqzgk,yw->hqyzgwk", f.reshape(NH, NQ, RZ, NGY, BK), eye_y)
    kz = kz.reshape(NH, NQ * GY * RZ, NGY * GY * BK)
    kzi = np.einsum("hqzgk,yw->hgykqwz", i.reshape(NH, NQ, RZ, NGY, BK), eye_y)
    kzi = kzi.reshape(NH, NGY * GY * BK, NQ * GY * RZ)
    ky = np.einsum("yb,kj->ykjb", f, eye_k).reshape(LEN * BK, BK * KM)
    kyi = np.einsum("yb,kj->kbyj", i, eye_k).reshape(BK * KM, LEN * BK)
    return tuple(np.ascontiguousarray(t).astype(ml_dtypes.bfloat16) for t in (ex, ix, kz, kzi, ky, kyi))


def iota(shape, axis):
    return lax.broadcasted_iota(jnp.int32, shape, axis)


def dot(a, b):
    return jnp.dot(a, b, preferred_element_type=F32)


def dot_nt(a, b):
    return lax.dot_general(a, b, (((1,), (1,)), ((), ())), preferred_element_type=F32)


def peer(place, off, ring):
    return (place // 2 + off // 2) % ring * 2 + (place + off) % 2


def swap_rows(first, second):
    low = iota(first.shape, 1) < BA
    return (
        jnp.where(low, first, pltpu.roll(second, BA, 1)),
        jnp.where(low, pltpu.roll(first, BA, 1), second),
    )


def swap_lanes(first, second):
    axis = first.ndim - 1
    low = iota(first.shape, axis) < 64
    return (
        jnp.where(low, first, pltpu.roll(second, 64, axis)),
        jnp.where(low, pltpu.roll(first, 64, axis), second),
    )


def gelu(x):
    inner = x * (math.sqrt(2.0 / math.pi) + (math.sqrt(2.0 / math.pi) * 0.044715) * (x * x))
    half = 0.5 * x
    return half + half * jnp.tanh(inner)


def kernel(
    forcing, lift_w, lift_b, point_w, spec_w, mixing, iterate, prev_it, prev_res,
    ex, ix, kz_all, kzi_all, ky_hbm, kyi_hbm,
    out, weights_out,
    v, pit, pres, step, forc, wts, lhs, xs, xr, xsa, xra, bs, br, gs, gr, gsa, gra, hs, hg,
    kz, kzi, ky, kyi, qm, qt, qa, mo, osc0, osc1, acc, ar1, ar2, ones,
    load_sem, in_sem, out_sem, loc_sem,
    xs_sem, xr_sem, xas_sem, xar_sem, bs_sem, br_sem, gs_sem, gr_sem, gas_sem, gar_sem, hs_sem, hr_sem,
    s1_sem, r1_sem, s2_sem, r2_sem,
):
    gy = lax.axis_index("gy")
    gz = lax.axis_index("gz")
    h = gz // NQ
    q = gz % NQ
    q_to = {off: peer(q, off, NQ // 2) for off in QPEERS}
    q_gz = {off: h * NQ + q_to[off] for off in QPEERS}
    y_to = {off: peer(gy, off, NGY // 2) for off in range(NGY)}
    h_to = [h, 1 - h]
    h_gz = [gz, (1 - h) * NQ + q]

    barrier = pltpu.get_barrier_semaphore()
    for dh, off in PEERS:
        pl.semaphore_signal(barrier, inc=1, device_id=(y_to[off], h_gz[dh]), device_id_type=MESH)
    for off in QPEERS:
        pl.semaphore_signal(barrier, inc=1, device_id=(gy, q_gz[off]), device_id_type=MESH)

    in_copies = [
        pltpu.make_async_copy(
            iterate.at[:, pl.ds(g * GY, GY)], v.at[:, pl.ds(g * GY, GY)], in_sem.at[g]
        )
        for g in range(GROUPS)
    ]
    loads = {
        name: pltpu.make_async_copy(src, dst, load_sem.at[n])
        for n, (name, src, dst) in enumerate([
            ("kz", kz_all.at[h], kz),
            ("pres", prev_res, pres),
            ("pit", prev_it, pit),
            ("ky", ky_hbm, ky),
            ("wts", spec_w, wts),
            ("kyi", kyi_hbm, kyi),
            ("kzi", kzi_all.at[h], kzi),
            ("forc", forcing, forc),
        ])
    }
    for copy in in_copies:
        copy.start()

    def to_q(src, dst, send_sem, recv_sem):
        def one(g, off):
            return pltpu.make_async_remote_copy(
                src.at[g, q_to[off]], dst.at[g, q], send_sem.at[g, off], recv_sem.at[g, off],
                device_id=(gy, q_gz[off]), device_id_type=MESH)
        return one

    send_x = to_q(xs, xr, xs_sem, xr_sem)
    send_a = to_q(xsa, xra, xas_sem, xar_sem)
    send_b = to_q(bs, br, bs_sem, br_sem)

    def to_g(src, dst, send_sem, recv_sem):
        def one(p, dh, off):
            return pltpu.make_async_remote_copy(
                src.at[p, h_to[dh], y_to[off]], dst.at[p, h, gy],
                send_sem.at[p, dh, off], recv_sem.at[p, dh, off],
                device_id=(y_to[off], h_gz[dh]), device_id_type=MESH)
        return one

    send_g = to_g(gs, gr, gs_sem, gr_sem)
    send_ga = to_g(gsa, gra, gas_sem, gar_sem)

    def send_h(p, dh, off):
        return pltpu.make_async_remote_copy(
            hs.at[p, y_to[off]], hg.at[p, h, gy], hs_sem.at[p, dh, off], hr_sem.at[p, dh, off],
            device_id=(y_to[off], h_gz[dh]), device_id_type=MESH)

    def own_x(g):
        return pltpu.make_async_copy(xs.at[g, q], xr.at[g, q], loc_sem.at[g])

    def own_a(g):
        return pltpu.make_async_copy(xsa.at[g, q], xra.at[g, q], loc_sem.at[4 + g])

    def own_b(g):
        return pltpu.make_async_copy(bs.at[g, q], br.at[g, q], loc_sem.at[8 + g])

    def own_g(p):
        return pltpu.make_async_copy(gs.at[p, h, gy], gr.at[p, h, gy], loc_sem.at[12 + p])

    def own_ga(p):
        return pltpu.make_async_copy(gsa.at[p, h, gy], gra.at[p, h, gy], loc_sem.at[16 + p])

    def own_h(p):
        return pltpu.make_async_copy(hs.at[p, gy], hg.at[p, h, gy], loc_sem.at[20 + p])

    def x_stage(g, field, dst):
        for pair in range(C // 2):
            parts = []
            for j in range(2):
                rows = field(2 * pair + j, pl.ds(g * GY, GY)).reshape(GY * RZ, LEN)
                parts.append(dot_nt(ex[...], rows).reshape(NQ, NH * BA, GY * RZ))
            dst[g, :, pair * 16:(pair + 1) * 16, :] = jnp.concatenate(parts, axis=1).astype(BF)

    def field_x(c, ys):
        return v[c, ys]

    def field_a(c, ys):
        return (pit[c, ys].astype(F32) + mixing[c] * pres[c, ys].astype(F32)).astype(BF)

    def field_b(c, ys):
        return step[c, ys].astype(BF)

    def z_stage(g, src, dst):
        left = jnp.concatenate([src[g, s] for s in range(NQ)], axis=1)
        part = dot(left, kz[...]).reshape(C // 2, 2, 8, 512)
        halves = swap_rows(part[:, 0], part[:, 1])
        for half in range(NH):
            block = halves[half].reshape(HALF, 512)
            for j in range(4):
                cut = block[:, j * 128:(j + 1) * 128]
                even, odd = swap_lanes(cut[:WIDE], cut[HALF - WIDE:])
                dst[g, half, 2 * j] = even.astype(BF)
                dst[g, half, 2 * j + 1] = odd.astype(BF)

    def unfold(first, second):
        top, bottom = swap_lanes(first, second)
        return jnp.concatenate([top, bottom[2 * WIDE - HALF:]], axis=0)

    def y_stage(src):
        parts = []
        for s in range(NGY):
            for p in range(2):
                pair = [src[g, 0, s].astype(F32) + src[g, 1, s].astype(F32) for g in (2 * p, 2 * p + 1)]
                parts.append(unfold(*pair).astype(BF))
        return dot(jnp.concatenate(parts, axis=1), ky[...])

    def mix_stage(sums):
        modes = sums.astype(BF).astype(F32).reshape(C // 2, 8, 512)
        for m in range(4):
            here = modes[:, :, m * 128:(m + 1) * 128]
            there = pltpu.roll(here, BA, 1)
            even, odd = swap_lanes(here, there)
            qm[2 * m * HALF:(2 * m + 1) * HALF, :] = even.reshape(HALF, 128)
            qm[(2 * m + 1) * HALF:(2 * m + 2) * HALF, :] = odd.reshape(HALF, 128)
        for a in range(BA):
            for t in range(C // 2):
                qt[a, t] = qm[pl.ds(t * 8 + a, BK, stride=HALF), :]

        def one(o, carry):
            for a in range(BA):
                total = jnp.zeros((BK, 128), F32)
                for t in range(C // 2):
                    total = total + wts[a, o, :, t * 128:(t + 1) * 128].astype(F32) * qt[a, t]
                row = pl.multiple_of((o * BA + a) * BK, BK)
                mo[pl.ds(row, BK), :] = total + pltpu.roll(total, 64, 1)
            return carry

        lax.fori_loop(0, C, one, 0, unroll=4)

    def yi_stage():
        low = iota((HALF, 128), 1) < 64
        left = jnp.concatenate(
            [jnp.where(low, mo[pl.ds(2 * m, HALF, stride=BK), :], mo[pl.ds(2 * m + 1, HALF, stride=BK), :])
             for m in range(4)], axis=1).astype(BF)
        for s in range(NGY):
            back = dot(left, kyi[:, s * 256:(s + 1) * 256])
            for p in range(2):
                cut = back[:, p * 128:(p + 1) * 128]
                even, odd = swap_lanes(cut[:WIDE], cut[HALF - WIDE:])
                hs[2 * p, s] = even.astype(BF)
                hs[2 * p + 1, s] = odd.astype(BF)

    def zi_stage(g):
        halves = [
            jnp.concatenate(
                [unfold(hg[g, half, 2 * j].astype(F32), hg[g, half, 2 * j + 1].astype(F32)) for j in range(4)],
                axis=1).reshape(C // 2, 8, 512)
            for half in range(NH)
        ]
        even, odd = swap_rows(*halves)
        left = jnp.concatenate([even, odd], axis=1).reshape(ROWS, 512).astype(BF)
        for s in range(0, NQ, 2):
            back = dot(left, kzi[:, s * 128:(s + 2) * 128]).astype(BF)
            bs[g, s] = back[:, :128]
            bs[g, s + 1] = back[:, 128:]

    def build_lhs():
        rows_o = iota((C * RZ, C), 0) // RZ
        pick = jnp.where(rows_o == iota((C * RZ, C), 1), 1.0, 0.0).astype(BF)
        col = iota((C, C * RZ), 1) // RZ
        spread = jnp.where(col == iota((C, C * RZ), 0), 1.0, 0.0).astype(BF)
        wide = dot(dot(pick, point_w[...]).astype(BF), spread)
        same = iota((C * RZ, C * RZ), 0) % RZ == iota((C * RZ, C * RZ), 1) % RZ
        wide = jnp.where(same, wide, 0.0)
        col3 = iota((3, 3 * RZ), 1) // RZ
        spread3 = jnp.where(col3 == iota((3, 3 * RZ), 0), 1.0, 0.0).astype(BF)
        lift = dot(dot_nt(pick, lift_w[...]).astype(BF), spread3)
        same3 = iota((C * RZ, 3 * RZ), 0) % RZ == iota((C * RZ, 3 * RZ), 1) % RZ
        lift = jnp.where(same3, lift, 0.0)
        bias = lift_b[...]
        hi = bias.astype(BF).astype(F32)
        mid = (bias - hi).astype(BF).astype(F32)
        lo = (bias - hi - mid).astype(BF).astype(F32)
        row = iota((16, C), 0)
        pieces = jnp.where(row == 0, hi, jnp.where(row == 1, mid, jnp.where(row == 2, lo, 0.0)))
        bias_cols = dot_nt(pick, pieces.astype(BF))
        full = jnp.concatenate([wide, lift, bias_cols], axis=1).astype(BF)
        for y in range(GY):
            lhs[y, :, 0:384] = full
        ones[...] = jnp.ones((16, LEN), BF)

    def turn_stage(g):
        for pair in range(C // 2):
            tile = br[g, :, pair * 16:(pair + 1) * 16, :].astype(F32)
            for j in range(2):
                block = tile[:, 8 * j:8 * j + 8].reshape(KM, GY * RZ)
                turned = jnp.transpose(block, (1, 0)).astype(BF).reshape(GY, RZ, KM)
                o = 2 * pair + j
                lhs[:, o * RZ:(o + 1) * RZ, 384:448] = turned

    def field_row(y):
        return v[:, y].reshape(C * RZ, LEN)

    def pre_activation(yl, y, dst):
        right = jnp.concatenate(
            [field_row(y), forc[:, y].reshape(3 * RZ, LEN), ones[...], ix[...]], axis=0)
        dst[...] = dot(lhs[yl][:, :448], right)

    def row_first(y, src):
        s_oo = jnp.zeros((RZ, LEN), F32)
        s_on = jnp.zeros((RZ, LEN), F32)
        s_nn = jnp.zeros((RZ, LEN), F32)
        for o in range(C):
            current = v[o, y].astype(F32)
            earlier = pres[o, y].astype(F32)
            newest = gelu(src[o * RZ:(o + 1) * RZ, :]) - current
            step[o, y] = current + mixing[o] * newest
            s_oo += earlier * earlier
            s_on += earlier * newest
            s_nn += newest * newest
        acc[0] += s_oo
        acc[1] += s_on
        acc[2] += s_nn

    def row_second(y, src):
        for o in range(C):
            current = v[o, y].astype(F32)
            pres[o, y] = (gelu(src[o * RZ:(o + 1) * RZ, :]) - current).astype(BF)

    def final(g, row):
        turn_stage(g)
        pre_activation(0, g * GY, osc0)

        def two_rows(i, carry):
            yl = 2 * i
            y = g * GY + yl
            pre_activation(yl + 1, y + 1, osc1)
            row(y, osc0)
            later = (yl + 2) % GY
            pre_activation(later, g * GY + later, osc0)
            row(y + 1, osc1)
            return carry

        lax.fori_loop(0, GY // 2, two_rows, 0)

    def combine(g, w_old, w_new):
        def one(c, carry):
            ys = pl.ds(g * GY, GY)
            old = pit[c, ys].astype(F32) + mixing[c] * pres[c, ys].astype(F32)
            v[c, ys] = (w_old * old + w_new * step[c, ys]).astype(BF)
            return carry

        lax.fori_loop(0, C, one, 0)

    def send_n1(off):
        return pltpu.make_async_remote_copy(
            ar1.at[q], ar1.at[q], s1_sem.at[off], r1_sem.at[off],
            device_id=(gy, q_gz[off]), device_id_type=MESH)

    def send_n2(dh, off):
        return pltpu.make_async_remote_copy(
            ar2.at[h, gy], ar2.at[h, gy], s2_sem.at[dh, off], r2_sem.at[dh, off],
            device_id=(y_to[off], h_gz[dh]), device_id_type=MESH)

    def start_norms():
        rows = iota((8, 128), 0)
        mine = jnp.zeros((8, 128), F32)
        for n in range(3):
            total = jnp.sum(acc[n], axis=0, keepdims=True)
            mine = jnp.where(rows == n, total[:, :128] + total[:, 128:], mine)
        ar2[h, gy] = mine
        for dh, off in PEERS:
            send_n2(dh, off).start()

    def next_norms():
        for dh, off in PEERS:
            send_n2(dh, off).wait_recv()
        total = jnp.zeros((8, 128), F32)
        for half in range(NH):
            for s in range(NGY):
                total = total + ar2[half, s]
        ar1[q] = total
        for off in QPEERS:
            send_n1(off).start()

    def end_norms():
        for off in QPEERS:
            send_n1(off).wait_recv()
        total = ar1[0]
        for s in range(1, NQ):
            total = total + ar1[s]
        sums = jnp.sum(total, axis=1, keepdims=True)
        norm_old, cross, norm_new = sums[0:1], sums[1:2], sums[2:3]
        ridge = REG * (norm_old + norm_new) + EPS
        denominator = norm_old + norm_new - 2.0 * cross + 2.0 * ridge
        w_old = (norm_new + ridge - cross) / denominator
        w_new = (norm_old + ridge - cross) / denominator
        weights_out[0] = w_old[0, 0]
        weights_out[1] = w_new[0, 0]
        return w_old, w_new

    def x_part(g):
        for off in QPEERS:
            send_x(g, off).start()
        own_x(g).start()

    def a_send(g):
        for off in QPEERS:
            send_a(g, off).start()
        own_a(g).start()

    def b_part(g):
        for off in QPEERS:
            send_x(g, off).wait_send()
        x_stage(g, field_b, xs)
        x_part(g)

    def z_part(g):
        own_x(g).wait()
        for off in QPEERS:
            send_x(g, off).wait_recv()
        z_stage(g, xr, gs)
        for dh, off in PEERS:
            send_g(g, dh, off).start()
        own_g(g).start()

    def za_part(g):
        own_a(g).wait()
        for off in QPEERS:
            send_a(g, off).wait_recv()
        z_stage(g, xra, gsa)
        for dh, off in PEERS:
            send_ga(g, dh, off).start()
        own_ga(g).start()

    def g_wait():
        for p in range(GROUPS):
            own_g(p).wait()
            for dh, off in PEERS:
                send_g(p, dh, off).wait_recv()

    def g_sent():
        for p in range(GROUPS):
            for dh, off in PEERS:
                send_g(p, dh, off).wait_send()

    def ga_wait():
        for p in range(GROUPS):
            own_ga(p).wait()
            for dh, off in PEERS:
                send_ga(p, dh, off).wait_recv()

    def h_part():
        yi_stage()
        h_send(0)
        h_send(1)

    def h_send(p):
        for dh, off in PEERS:
            send_h(p, dh, off).start()
        own_h(p).start()

    def zi_part(p):
        own_h(p).wait()
        for dh, off in PEERS:
            send_h(p, dh, off).wait_recv()
        zi_stage(p)
        for off in QPEERS:
            send_b(p, off).start()
        own_b(p).start()

    def b_wait(g):
        own_b(g).wait()
        for off in QPEERS:
            send_b(g, off).wait_recv()

    def inverse_sent():
        for p in range(GROUPS):
            for dh, off in PEERS:
                send_h(p, dh, off).wait_send()
        for g in range(GROUPS):
            for off in QPEERS:
                send_b(g, off).wait_send()

    for g in range(GROUPS):
        in_copies[g].wait()
        if g == 2:
            loads["kz"].start()
        x_stage(g, field_x, xs)
        if g == 0:
            pl.semaphore_wait(barrier, len(PEERS) + len(QPEERS))
        x_part(g)
    for name, copy in loads.items():
        if name != "kz":
            copy.start()
    acc[...] = jnp.zeros((3, RZ, LEN), F32)
    build_lhs()
    loads["kz"].wait()
    z_part(0)
    loads["pres"].wait()
    loads["pit"].wait()
    for g in range(1, GROUPS):
        x_stage(g - 1, field_a, xsa)
        z_part(g)
    for g in range(GROUPS - 1):
        a_send(g)
    x_stage(GROUPS - 1, field_a, xsa)
    a_send(GROUPS - 1)
    for name in ("ky", "wts", "kyi", "kzi", "forc"):
        loads[name].wait()
    g_wait()
    mix_stage(y_stage(gr))
    h_part()
    h_send(2)
    h_send(3)
    for g in range(GROUPS):
        zi_part(g)
    g_sent()
    za_part(0)
    za_part(1)
    b_wait(0)
    final(0, row_first)
    b_part(0)
    za_part(2)
    za_part(3)
    for g in range(1, GROUPS):
        b_wait(g)
        final(g, row_first)
        if g == GROUPS - 1:
            start_norms()
        b_part(g)
    inverse_sent()

    z_part(0)
    z_part(1)
    next_norms()
    ga_wait()
    qa[...] = y_stage(gra)
    z_part(2)
    z_part(3)
    w_old, w_new = end_norms()
    g_wait()
    mix_stage(w_old * qa[...] + w_new * y_stage(gr))
    h_part()
    parts = (w_old.reshape(1, 1, 1), w_new.reshape(1, 1, 1))
    combine(0, *parts)
    h_send(2)
    combine(1, *parts)
    h_send(3)
    for g in range(GROUPS):
        zi_part(g)
    combine(2, *parts)
    combine(3, *parts)
    out_copies = []
    for g in range(GROUPS):
        b_wait(g)
        final(g, row_second)
        ys = pl.ds(g * GY, GY)
        out_copies.append(pltpu.make_async_copy(pres.at[:, ys], out.at[:, ys], out_sem.at[g]))
        out_copies[-1].start()
    for off in QPEERS:
        send_n1(off).wait_send()
    for dh, off in PEERS:
        send_n2(dh, off).wait_send()
    for g in range(GROUPS):
        for off in QPEERS:
            send_x(g, off).wait_send()
            send_a(g, off).wait_send()
    g_sent()
    for p in range(GROUPS):
        for dh, off in PEERS:
            send_ga(p, dh, off).wait_send()
    inverse_sent()
    for copy in out_copies:
        copy.wait()


def shards(forcing, lift_weight, lift_bias, point_weight, spectral_weight, mixing, iterate, prev_iterate, prev_residual):
    ex, ix, kz, kzi, ky, kyi = (jnp.asarray(t) for t in tables())
    field = (C, RY, RZ, LEN)
    vmem = pl.BlockSpec(memory_space=pltpu.VMEM)
    smem = pl.BlockSpec(memory_space=pltpu.SMEM)
    hbm = pl.BlockSpec(memory_space=pl.ANY)
    dma = pltpu.SemaphoreType.DMA
    scratch = [
        pltpu.VMEM(field, BF),
        pltpu.VMEM(field, BF),
        pltpu.VMEM(field, BF),
        pltpu.VMEM(field, F32),
        pltpu.VMEM((3, RY, RZ, LEN), BF),
        pltpu.VMEM((BA, C, BK, C * KM), BF),
        pltpu.VMEM((GY, C * RZ, 512), BF),
        pltpu.VMEM((GROUPS, NQ, ROWS, 128), BF),
        pltpu.VMEM((GROUPS, NQ, ROWS, 128), BF),
        pltpu.VMEM((GROUPS, NQ, ROWS, 128), BF),
        pltpu.VMEM((GROUPS, NQ, ROWS, 128), BF),
        pltpu.VMEM((GROUPS, NQ, ROWS, 128), BF),
        pltpu.VMEM((GROUPS, NQ, ROWS, 128), BF),
        pltpu.VMEM((GROUPS, NH, NGY, WIDE, 128), BF),
        pltpu.VMEM((GROUPS, NH, NGY, WIDE, 128), BF),
        pltpu.VMEM((GROUPS, NH, NGY, WIDE, 128), BF),
        pltpu.VMEM((GROUPS, NH, NGY, WIDE, 128), BF),
        pltpu.VMEM((GROUPS, NGY, WIDE, 128), BF),
        pltpu.VMEM((GROUPS, NH, NGY, WIDE, 128), BF),
        pltpu.VMEM((1024, 512), BF),
        pltpu.VMEM((512, 1024), BF),
        pltpu.VMEM((2048, 512), BF),
        pltpu.VMEM((512, 2048), BF),
        pltpu.VMEM((BK * HALF, 128), F32),
        pltpu.VMEM((BA, C // 2, BK, 128), F32),
        pltpu.VMEM((HALF, 512), F32),
        pltpu.VMEM((BK * HALF, 128), F32),
        pltpu.VMEM((C * RZ, LEN), F32),
        pltpu.VMEM((C * RZ, LEN), F32),
        pltpu.VMEM((3, RZ, LEN), F32),
        pltpu.VMEM((NQ, 8, 128), F32),
        pltpu.VMEM((NH, NGY, 8, 128), F32),
        pltpu.VMEM((16, LEN), BF),
        dma((8,)), dma((GROUPS,)), dma((GROUPS,)), dma((24,)),
        dma((GROUPS, NQ)), dma((GROUPS, NQ)), dma((GROUPS, NQ)), dma((GROUPS, NQ)),
        dma((GROUPS, NQ)), dma((GROUPS, NQ)),
        dma((GROUPS, NH, NGY)), dma((GROUPS, NH, NGY)), dma((GROUPS, NH, NGY)), dma((GROUPS, NH, NGY)),
        dma((GROUPS, NH, NGY)), dma((GROUPS, NH, NGY)),
        dma((NQ,)), dma((NQ,)), dma((NH, NGY)), dma((NH, NGY)),
    ]
    result, weights = pl.pallas_call(
        kernel,
        out_shape=(
            jax.ShapeDtypeStruct(field, BF),
            jax.ShapeDtypeStruct((2,), F32),
        ),
        in_specs=[hbm, vmem, vmem, vmem, hbm, smem, hbm, hbm, hbm, vmem, vmem, hbm, hbm, hbm, hbm],
        out_specs=(hbm, smem),
        scratch_shapes=scratch,
        compiler_params=pltpu.CompilerParams(
            collective_id=0, has_side_effects=True, vmem_limit_bytes=60 * 1024 * 1024),
        cost_estimate=pl.CostEstimate(
            flops=10_000_000_000, bytes_accessed=40_000_000, transcendentals=5_000_000),
    )(forcing, lift_weight.T, lift_bias.reshape(1, C), point_weight,
      jnp.transpose(spectral_weight, (0, 2, 1, 3)), mixing,
      iterate, prev_iterate, prev_residual, ex, ix, kz, kzi, ky, kyi)
    return result, weights


def solution(mesh):
    in_specs = (
        P(None, "gy", "gz", None),
        P(),
        P(),
        P(),
        P("gz", "gy", None, None),
        P(),
        P(None, "gy", "gz", None),
        P(None, "gy", "gz", None),
        P(None, "gy", "gz", None),
    )
    out_specs = (P(None, "gy", "gz", None), P())
    return jax.shard_map(shards, mesh=mesh, in_specs=in_specs, out_specs=out_specs, check_vma=False)
```

```python
import functools
import math

import jax
import jax.numpy as jnp
import ml_dtypes
import numpy as np
from jax import lax
from jax.experimental import pallas as pl
from jax.experimental.pallas import tpu as pltpu
from jax.sharding import PartitionSpec as P

MESH = pl.DeviceIdType.MESH
BF = jnp.bfloat16
F32 = jnp.float32

MODES = 32
KM = 64
REG = 0.001
EPS = 1e-06

C = 20
LEN = 256
NGY = 8
NQ = 8
NH = 2
RY = 32
RZ = 16
GROUPS = 4
GY = 8
BA = 4
BK = 8
ROWS = C * NH * BA
HALF = C * BA


WIDE = 48


def ring_steps(off, ring):
    return min(off // 2, ring - off // 2)


PEERS = sorted(
    [(dh, off) for off in range(NGY) for dh in range(NH) if (dh, off) != (0, 0)],
    key=lambda t: -(ring_steps(t[1], NGY // 2) + (1 if t[1] % 2 else 2 * t[0])))
QPEERS = sorted(range(1, NQ), key=lambda t: -ring_steps(t, NQ // 2))


def dft_table(length):
    positions = np.arange(length)[:, None]
    waves = np.arange(2 * MODES)[None, :]
    number = np.where(waves < MODES, waves, waves - MODES + 1)
    angles = (positions * number % length).astype(np.float32) * np.float32(2.0 * math.pi / length)
    both = np.where(waves < MODES, np.cos(angles), np.sin(angles)).astype(np.float32)
    inverse = (both * np.float32(2.0 / length)).astype(ml_dtypes.bfloat16)
    return both.astype(ml_dtypes.bfloat16), inverse


@functools.lru_cache(maxsize=None)
def tables():
    fwd, inv = dft_table(LEN)
    f = fwd.astype(np.float32)
    i = inv.astype(np.float32)
    order = np.arange(KM).reshape(NH, NQ, BA).transpose(1, 0, 2).reshape(-1)
    ex = f[:, order].T
    ix = i[:, order].T
    eye_y = np.eye(GY, dtype=np.float32)
    eye_k = np.eye(BK, dtype=np.float32)
    kz = np.einsum("hqzgk,yw->hqyzgwk", f.reshape(NH, NQ, RZ, NGY, BK), eye_y)
    kz = kz.reshape(NH, NQ * GY * RZ, NGY * GY * BK)
    kzi = np.einsum("hqzgk,yw->hgykqwz", i.reshape(NH, NQ, RZ, NGY, BK), eye_y)
    kzi = kzi.reshape(NH, NGY * GY * BK, NQ * GY * RZ)
    ky = np.einsum("yb,kj->ykjb", f, eye_k).reshape(LEN * BK, BK * KM)
    kyi = np.einsum("yb,kj->kbyj", i, eye_k).reshape(BK * KM, LEN * BK)
    return tuple(np.ascontiguousarray(t).astype(ml_dtypes.bfloat16) for t in (ex, ix, kz, kzi, ky, kyi))


def iota(shape, axis):
    return lax.broadcasted_iota(jnp.int32, shape, axis)


def dot(a, b):
    return jnp.dot(a, b, preferred_element_type=F32)


def dot_nt(a, b):
    return lax.dot_general(a, b, (((1,), (1,)), ((), ())), preferred_element_type=F32)


def peer(place, off, ring):
    return (place // 2 + off // 2) % ring * 2 + (place + off) % 2


def swap_rows(first, second):
    low = iota(first.shape, 1) < BA
    return (
        jnp.where(low, first, pltpu.roll(second, BA, 1)),
        jnp.where(low, pltpu.roll(first, BA, 1), second),
    )


def swap_lanes(first, second):
    axis = first.ndim - 1
    low = iota(first.shape, axis) < 64
    return (
        jnp.where(low, first, pltpu.roll(second, 64, axis)),
        jnp.where(low, pltpu.roll(first, 64, axis), second),
    )


def gelu(x):
    inner = x * (math.sqrt(2.0 / math.pi) + (math.sqrt(2.0 / math.pi) * 0.044715) * (x * x))
    half = 0.5 * x
    return half + half * jnp.tanh(inner)


def kernel(
    forcing, lift_w, lift_b, point_w, spec_w, mixing, iterate, prev_it, prev_res,
    ex, ix, kz_all, kzi_all, ky_hbm, kyi_hbm,
    out, weights_out,
    v, pit, pres, step, forc, wts, lhs, xs, xr, xsa, xra, bs, br, gs, gr, gsa, gra, hs, hg,
    kz, kzi, ky, kyi, qm, qt, qa, mo, osc0, osc1, acc, ar1, ar2, ones,
    load_sem, in_sem, out_sem, loc_sem,
    xs_sem, xr_sem, xas_sem, xar_sem, bs_sem, br_sem, gs_sem, gr_sem, gas_sem, gar_sem, hs_sem, hr_sem,
    s1_sem, r1_sem, s2_sem, r2_sem,
):
    gy = lax.axis_index("gy")
    gz = lax.axis_index("gz")
    h = gz // NQ
    q = gz % NQ
    q_to = {off: peer(q, off, NQ // 2) for off in QPEERS}
    q_gz = {off: h * NQ + q_to[off] for off in QPEERS}
    y_to = {off: peer(gy, off, NGY // 2) for off in range(NGY)}
    h_to = [h, 1 - h]
    h_gz = [gz, (1 - h) * NQ + q]

    barrier = pltpu.get_barrier_semaphore()
    for dh, off in PEERS:
        pl.semaphore_signal(barrier, inc=1, device_id=(y_to[off], h_gz[dh]), device_id_type=MESH)
    for off in QPEERS:
        pl.semaphore_signal(barrier, inc=1, device_id=(gy, q_gz[off]), device_id_type=MESH)

    in_copies = [
        pltpu.make_async_copy(
            iterate.at[:, pl.ds(g * GY, GY)], v.at[:, pl.ds(g * GY, GY)], in_sem.at[g]
        )
        for g in range(GROUPS)
    ]
    loads = {
        name: pltpu.make_async_copy(src, dst, load_sem.at[n])
        for n, (name, src, dst) in enumerate([
            ("kz", kz_all.at[h], kz),
            ("pres", prev_res, pres),
            ("pit", prev_it, pit),
            ("ky", ky_hbm, ky),
            ("wts", spec_w, wts),
            ("kyi", kyi_hbm, kyi),
            ("kzi", kzi_all.at[h], kzi),
            ("forc", forcing, forc),
        ])
    }
    for copy in in_copies:
        copy.start()

    def to_q(src, dst, send_sem, recv_sem):
        def one(g, off):
            return pltpu.make_async_remote_copy(
                src.at[g, q_to[off]], dst.at[g, q], send_sem.at[g, off], recv_sem.at[g, off],
                device_id=(gy, q_gz[off]), device_id_type=MESH)
        return one

    send_x = to_q(xs, xr, xs_sem, xr_sem)
    send_a = to_q(xsa, xra, xas_sem, xar_sem)
    send_b = to_q(bs, br, bs_sem, br_sem)

    def to_g(src, dst, send_sem, recv_sem):
        def one(p, dh, off):
            return pltpu.make_async_remote_copy(
                src.at[p, h_to[dh], y_to[off]], dst.at[p, h, gy],
                send_sem.at[p, dh, off], recv_sem.at[p, dh, off],
                device_id=(y_to[off], h_gz[dh]), device_id_type=MESH)
        return one

    send_g = to_g(gs, gr, gs_sem, gr_sem)
    send_ga = to_g(gsa, gra, gas_sem, gar_sem)

    def send_h(p, dh, off):
        return pltpu.make_async_remote_copy(
            hs.at[p, y_to[off]], hg.at[p, h, gy], hs_sem.at[p, dh, off], hr_sem.at[p, dh, off],
            device_id=(y_to[off], h_gz[dh]), device_id_type=MESH)

    def own_x(g):
        return pltpu.make_async_copy(xs.at[g, q], xr.at[g, q], loc_sem.at[g])

    def own_a(g):
        return pltpu.make_async_copy(xsa.at[g, q], xra.at[g, q], loc_sem.at[4 + g])

    def own_b(g):
        return pltpu.make_async_copy(bs.at[g, q], br.at[g, q], loc_sem.at[8 + g])

    def own_g(p):
        return pltpu.make_async_copy(gs.at[p, h, gy], gr.at[p, h, gy], loc_sem.at[12 + p])

    def own_ga(p):
        return pltpu.make_async_copy(gsa.at[p, h, gy], gra.at[p, h, gy], loc_sem.at[16 + p])

    def own_h(p):
        return pltpu.make_async_copy(hs.at[p, gy], hg.at[p, h, gy], loc_sem.at[20 + p])

    def x_stage(g, field, dst):
        for pair in range(C // 2):
            parts = []
            for j in range(2):
                rows = field(2 * pair + j, pl.ds(g * GY, GY)).reshape(GY * RZ, LEN)
                parts.append(dot_nt(ex[...], rows).reshape(NQ, NH * BA, GY * RZ))
            dst[g, :, pair * 16:(pair + 1) * 16, :] = jnp.concatenate(parts, axis=1).astype(BF)

    def field_x(c, ys):
        return v[c, ys]

    def field_a(c, ys):
        return (pit[c, ys].astype(F32) + mixing[c] * pres[c, ys].astype(F32)).astype(BF)

    def field_b(c, ys):
        return step[c, ys].astype(BF)

    def z_stage(g, src, dst):
        left = jnp.concatenate([src[g, s] for s in range(NQ)], axis=1)
        part = dot(left, kz[...]).reshape(C // 2, 2, 8, 512)
        halves = swap_rows(part[:, 0], part[:, 1])
        for half in range(NH):
            block = halves[half].reshape(HALF, 512)
            for j in range(4):
                cut = block[:, j * 128:(j + 1) * 128]
                even, odd = swap_lanes(cut[:WIDE], cut[HALF - WIDE:])
                dst[g, half, 2 * j] = even.astype(BF)
                dst[g, half, 2 * j + 1] = odd.astype(BF)

    def unfold(first, second):
        top, bottom = swap_lanes(first, second)
        return jnp.concatenate([top, bottom[2 * WIDE - HALF:]], axis=0)

    def y_stage(src):
        parts = []
        for s in range(NGY):
            for p in range(2):
                pair = [src[g, 0, s].astype(F32) + src[g, 1, s].astype(F32) for g in (2 * p, 2 * p + 1)]
                parts.append(unfold(*pair).astype(BF))
        return dot(jnp.concatenate(parts, axis=1), ky[...])

    def mix_stage(sums):
        modes = sums.astype(BF).astype(F32).reshape(C // 2, 8, 512)
        for m in range(4):
            here = modes[:, :, m * 128:(m + 1) * 128]
            there = pltpu.roll(here, BA, 1)
            even, odd = swap_lanes(here, there)
            qm[2 * m * HALF:(2 * m + 1) * HALF, :] = even.reshape(HALF, 128)
            qm[(2 * m + 1) * HALF:(2 * m + 2) * HALF, :] = odd.reshape(HALF, 128)
        for a in range(BA):
            for t in range(C // 2):
                qt[a, t] = qm[pl.ds(t * 8 + a, BK, stride=HALF), :]

        def one(o, carry):
            for a in range(BA):
                total = jnp.zeros((BK, 128), F32)
                for t in range(C // 2):
                    total = total + wts[a, o, :, t * 128:(t + 1) * 128].astype(F32) * qt[a, t]
                row = pl.multiple_of((o * BA + a) * BK, BK)
                mo[pl.ds(row, BK), :] = total + pltpu.roll(total, 64, 1)
            return carry

        lax.fori_loop(0, C, one, 0, unroll=4)

    def yi_stage():
        low = iota((HALF, 128), 1) < 64
        left = jnp.concatenate(
            [jnp.where(low, mo[pl.ds(2 * m, HALF, stride=BK), :], mo[pl.ds(2 * m + 1, HALF, stride=BK), :])
             for m in range(4)], axis=1).astype(BF)
        for s in range(NGY):
            back = dot(left, kyi[:, s * 256:(s + 1) * 256])
            for p in range(2):
                cut = back[:, p * 128:(p + 1) * 128]
                even, odd = swap_lanes(cut[:WIDE], cut[HALF - WIDE:])
                hs[2 * p, s] = even.astype(BF)
                hs[2 * p + 1, s] = odd.astype(BF)

    def zi_stage(g):
        halves = [
            jnp.concatenate(
                [unfold(hg[g, half, 2 * j].astype(F32), hg[g, half, 2 * j + 1].astype(F32)) for j in range(4)],
                axis=1).reshape(C // 2, 8, 512)
            for half in range(NH)
        ]
        even, odd = swap_rows(*halves)
        left = jnp.concatenate([even, odd], axis=1).reshape(ROWS, 512).astype(BF)
        for s in range(0, NQ, 2):
            back = dot(left, kzi[:, s * 128:(s + 2) * 128]).astype(BF)
            bs[g, s] = back[:, :128]
            bs[g, s + 1] = back[:, 128:]

    def build_lhs():
        rows_o = iota((C * RZ, C), 0) // RZ
        pick = jnp.where(rows_o == iota((C * RZ, C), 1), 1.0, 0.0).astype(BF)
        col = iota((C, C * RZ), 1) // RZ
        spread = jnp.where(col == iota((C, C * RZ), 0), 1.0, 0.0).astype(BF)
        wide = dot(dot(pick, point_w[...]).astype(BF), spread)
        same = iota((C * RZ, C * RZ), 0) % RZ == iota((C * RZ, C * RZ), 1) % RZ
        wide = jnp.where(same, wide, 0.0)
        col3 = iota((3, 3 * RZ), 1) // RZ
        spread3 = jnp.where(col3 == iota((3, 3 * RZ), 0), 1.0, 0.0).astype(BF)
        lift = dot(dot_nt(pick, lift_w[...]).astype(BF), spread3)
        same3 = iota((C * RZ, 3 * RZ), 0) % RZ == iota((C * RZ, 3 * RZ), 1) % RZ
        lift = jnp.where(same3, lift, 0.0)
        bias = lift_b[...]
        hi = bias.astype(BF).astype(F32)
        mid = (bias - hi).astype(BF).astype(F32)
        lo = (bias - hi - mid).astype(BF).astype(F32)
        row = iota((16, C), 0)
        pieces = jnp.where(row == 0, hi, jnp.where(row == 1, mid, jnp.where(row == 2, lo, 0.0)))
        bias_cols = dot_nt(pick, pieces.astype(BF))
        full = jnp.concatenate([wide, lift, bias_cols], axis=1).astype(BF)
        for y in range(GY):
            lhs[y, :, 0:384] = full
        ones[...] = jnp.ones((16, LEN), BF)

    def turn_stage(g):
        for pair in range(C // 2):
            tile = br[g, :, pair * 16:(pair + 1) * 16, :].astype(F32)
            for j in range(2):
                block = tile[:, 8 * j:8 * j + 8].reshape(KM, GY * RZ)
                turned = jnp.transpose(block, (1, 0)).astype(BF).reshape(GY, RZ, KM)
                o = 2 * pair + j
                lhs[:, o * RZ:(o + 1) * RZ, 384:448] = turned

    def field_row(y):
        return v[:, y].reshape(C * RZ, LEN)

    def pre_activation(yl, y, dst):
        right = jnp.concatenate(
            [field_row(y), forc[:, y].reshape(3 * RZ, LEN), ones[...], ix[...]], axis=0)
        dst[...] = dot(lhs[yl][:, :448], right)

    def row_first(y, src):
        s_oo = jnp.zeros((RZ, LEN), F32)
        s_on = jnp.zeros((RZ, LEN), F32)
        s_nn = jnp.zeros((RZ, LEN), F32)
        for o in range(C):
            current = v[o, y].astype(F32)
            earlier = pres[o, y].astype(F32)
            newest = gelu(src[o * RZ:(o + 1) * RZ, :]) - current
            step[o, y] = current + mixing[o] * newest
            s_oo += earlier * earlier
            s_on += earlier * newest
            s_nn += newest * newest
        acc[0] += s_oo
        acc[1] += s_on
        acc[2] += s_nn

    def row_second(y, src):
        for o in range(C):
            current = v[o, y].astype(F32)
            pres[o, y] = (gelu(src[o * RZ:(o + 1) * RZ, :]) - current).astype(BF)

    def final(g, row):
        turn_stage(g)
        pre_activation(0, g * GY, osc0)

        def two_rows(i, carry):
            yl = 2 * i
            y = g * GY + yl
            pre_activation(yl + 1, y + 1, osc1)
            row(y, osc0)
            later = (yl + 2) % GY
            pre_activation(later, g * GY + later, osc0)
            row(y + 1, osc1)
            return carry

        lax.fori_loop(0, GY // 2, two_rows, 0)

    def combine(g, w_old, w_new):
        def one(c, carry):
            ys = pl.ds(g * GY, GY)
            old = pit[c, ys].astype(F32) + mixing[c] * pres[c, ys].astype(F32)
            v[c, ys] = (w_old * old + w_new * step[c, ys]).astype(BF)
            return carry

        lax.fori_loop(0, C, one, 0)

    def send_n1(off):
        return pltpu.make_async_remote_copy(
            ar1.at[q], ar1.at[q], s1_sem.at[off], r1_sem.at[off],
            device_id=(gy, q_gz[off]), device_id_type=MESH)

    def send_n2(dh, off):
        return pltpu.make_async_remote_copy(
            ar2.at[h, gy], ar2.at[h, gy], s2_sem.at[dh, off], r2_sem.at[dh, off],
            device_id=(y_to[off], h_gz[dh]), device_id_type=MESH)

    def start_norms():
        rows = iota((8, 128), 0)
        mine = jnp.zeros((8, 128), F32)
        for n in range(3):
            total = jnp.sum(acc[n], axis=0, keepdims=True)
            mine = jnp.where(rows == n, total[:, :128] + total[:, 128:], mine)
        ar2[h, gy] = mine
        for dh, off in PEERS:
            send_n2(dh, off).start()

    def next_norms():
        for dh, off in PEERS:
            send_n2(dh, off).wait_recv()
        total = jnp.zeros((8, 128), F32)
        for half in range(NH):
            for s in range(NGY):
                total = total + ar2[half, s]
        ar1[q] = total
        for off in QPEERS:
            send_n1(off).start()

    def end_norms():
        for off in QPEERS:
            send_n1(off).wait_recv()
        total = ar1[0]
        for s in range(1, NQ):
            total = total + ar1[s]
        sums = jnp.sum(total, axis=1, keepdims=True)
        norm_old, cross, norm_new = sums[0:1], sums[1:2], sums[2:3]
        ridge = REG * (norm_old + norm_new) + EPS
        denominator = norm_old + norm_new - 2.0 * cross + 2.0 * ridge
        w_old = (norm_new + ridge - cross) / denominator
        w_new = (norm_old + ridge - cross) / denominator
        weights_out[0] = w_old[0, 0]
        weights_out[1] = w_new[0, 0]
        return w_old, w_new

    def x_part(g):
        for off in QPEERS:
            send_x(g, off).start()
        own_x(g).start()

    def a_send(g):
        for off in QPEERS:
            send_a(g, off).start()
        own_a(g).start()

    def b_part(g):
        for off in QPEERS:
            send_x(g, off).wait_send()
        x_stage(g, field_b, xs)
        x_part(g)

    def z_part(g):
        own_x(g).wait()
        for off in QPEERS:
            send_x(g, off).wait_recv()
        z_stage(g, xr, gs)
        for dh, off in PEERS:
            send_g(g, dh, off).start()
        own_g(g).start()

    def za_part(g):
        own_a(g).wait()
        for off in QPEERS:
            send_a(g, off).wait_recv()
        z_stage(g, xra, gsa)
        for dh, off in PEERS:
            send_ga(g, dh, off).start()
        own_ga(g).start()

    def g_wait():
        for p in range(GROUPS):
            own_g(p).wait()
            for dh, off in PEERS:
                send_g(p, dh, off).wait_recv()

    def g_sent():
        for p in range(GROUPS):
            for dh, off in PEERS:
                send_g(p, dh, off).wait_send()

    def ga_wait():
        for p in range(GROUPS):
            own_ga(p).wait()
            for dh, off in PEERS:
                send_ga(p, dh, off).wait_recv()

    def h_part():
        yi_stage()
        h_send(0)
        h_send(1)

    def h_send(p):
        for dh, off in PEERS:
            send_h(p, dh, off).start()
        own_h(p).start()

    def zi_part(p):
        own_h(p).wait()
        for dh, off in PEERS:
            send_h(p, dh, off).wait_recv()
        zi_stage(p)
        for off in QPEERS:
            send_b(p, off).start()
        own_b(p).start()

    def b_wait(g):
        own_b(g).wait()
        for off in QPEERS:
            send_b(g, off).wait_recv()

    def inverse_sent():
        for p in range(GROUPS):
            for dh, off in PEERS:
                send_h(p, dh, off).wait_send()
        for g in range(GROUPS):
            for off in QPEERS:
                send_b(g, off).wait_send()

    for g in range(GROUPS):
        in_copies[g].wait()
        if g == 2:
            loads["kz"].start()
        x_stage(g, field_x, xs)
        if g == 0:
            pl.semaphore_wait(barrier, len(PEERS) + len(QPEERS))
        x_part(g)
    for name, copy in loads.items():
        if name != "kz":
            copy.start()
    acc[...] = jnp.zeros((3, RZ, LEN), F32)
    build_lhs()
    loads["kz"].wait()
    z_part(0)
    loads["pres"].wait()
    loads["pit"].wait()
    for g in range(1, GROUPS):
        x_stage(g - 1, field_a, xsa)
        z_part(g)
    for g in range(GROUPS - 1):
        a_send(g)
    x_stage(GROUPS - 1, field_a, xsa)
    a_send(GROUPS - 1)
    for name in ("ky", "wts", "kyi", "kzi", "forc"):
        loads[name].wait()
    g_wait()
    mix_stage(y_stage(gr))
    h_part()
    h_send(2)
    h_send(3)
    za_part(0)
    za_part(1)
    for g in range(GROUPS):
        zi_part(g)
    g_sent()
    za_part(2)
    za_part(3)
    b_wait(0)
    final(0, row_first)
    b_part(0)
    for g in range(1, GROUPS):
        b_wait(g)
        final(g, row_first)
        if g == GROUPS - 1:
            start_norms()
        b_part(g)
    inverse_sent()

    z_part(0)
    z_part(1)
    next_norms()
    ga_wait()
    qa[...] = y_stage(gra)
    z_part(2)
    z_part(3)
    w_old, w_new = end_norms()
    g_wait()
    mix_stage(w_old * qa[...] + w_new * y_stage(gr))
    h_part()
    parts = (w_old.reshape(1, 1, 1), w_new.reshape(1, 1, 1))
    combine(0, *parts)
    h_send(2)
    combine(1, *parts)
    h_send(3)
    for g in range(GROUPS):
        zi_part(g)
    combine(2, *parts)
    combine(3, *parts)
    out_copies = []
    for g in range(GROUPS):
        b_wait(g)
        final(g, row_second)
        ys = pl.ds(g * GY, GY)
        out_copies.append(pltpu.make_async_copy(pres.at[:, ys], out.at[:, ys], out_sem.at[g]))
        out_copies[-1].start()
    for off in QPEERS:
        send_n1(off).wait_send()
    for dh, off in PEERS:
        send_n2(dh, off).wait_send()
    for g in range(GROUPS):
        for off in QPEERS:
            send_x(g, off).wait_send()
            send_a(g, off).wait_send()
    g_sent()
    for p in range(GROUPS):
        for dh, off in PEERS:
            send_ga(p, dh, off).wait_send()
    inverse_sent()
    for copy in out_copies:
        copy.wait()


def shards(forcing, lift_weight, lift_bias, point_weight, spectral_weight, mixing, iterate, prev_iterate, prev_residual):
    ex, ix, kz, kzi, ky, kyi = (jnp.asarray(t) for t in tables())
    field = (C, RY, RZ, LEN)
    vmem = pl.BlockSpec(memory_space=pltpu.VMEM)
    smem = pl.BlockSpec(memory_space=pltpu.SMEM)
    hbm = pl.BlockSpec(memory_space=pl.ANY)
    dma = pltpu.SemaphoreType.DMA
    scratch = [
        pltpu.VMEM(field, BF),
        pltpu.VMEM(field, BF),
        pltpu.VMEM(field, BF),
        pltpu.VMEM(field, F32),
        pltpu.VMEM((3, RY, RZ, LEN), BF),
        pltpu.VMEM((BA, C, BK, C * KM), BF),
        pltpu.VMEM((GY, C * RZ, 512), BF),
        pltpu.VMEM((GROUPS, NQ, ROWS, 128), BF),
        pltpu.VMEM((GROUPS, NQ, ROWS, 128), BF),
        pltpu.VMEM((GROUPS, NQ, ROWS, 128), BF),
        pltpu.VMEM((GROUPS, NQ, ROWS, 128), BF),
        pltpu.VMEM((GROUPS, NQ, ROWS, 128), BF),
        pltpu.VMEM((GROUPS, NQ, ROWS, 128), BF),
        pltpu.VMEM((GROUPS, NH, NGY, WIDE, 128), BF),
        pltpu.VMEM((GROUPS, NH, NGY, WIDE, 128), BF),
        pltpu.VMEM((GROUPS, NH, NGY, WIDE, 128), BF),
        pltpu.VMEM((GROUPS, NH, NGY, WIDE, 128), BF),
        pltpu.VMEM((GROUPS, NGY, WIDE, 128), BF),
        pltpu.VMEM((GROUPS, NH, NGY, WIDE, 128), BF),
        pltpu.VMEM((1024, 512), BF),
        pltpu.VMEM((512, 1024), BF),
        pltpu.VMEM((2048, 512), BF),
        pltpu.VMEM((512, 2048), BF),
        pltpu.VMEM((BK * HALF, 128), F32),
        pltpu.VMEM((BA, C // 2, BK, 128), F32),
        pltpu.VMEM((HALF, 512), F32),
        pltpu.VMEM((BK * HALF, 128), F32),
        pltpu.VMEM((C * RZ, LEN), F32),
        pltpu.VMEM((C * RZ, LEN), F32),
        pltpu.VMEM((3, RZ, LEN), F32),
        pltpu.VMEM((NQ, 8, 128), F32),
        pltpu.VMEM((NH, NGY, 8, 128), F32),
        pltpu.VMEM((16, LEN), BF),
        dma((8,)), dma((GROUPS,)), dma((GROUPS,)), dma((24,)),
        dma((GROUPS, NQ)), dma((GROUPS, NQ)), dma((GROUPS, NQ)), dma((GROUPS, NQ)),
        dma((GROUPS, NQ)), dma((GROUPS, NQ)),
        dma((GROUPS, NH, NGY)), dma((GROUPS, NH, NGY)), dma((GROUPS, NH, NGY)), dma((GROUPS, NH, NGY)),
        dma((GROUPS, NH, NGY)), dma((GROUPS, NH, NGY)),
        dma((NQ,)), dma((NQ,)), dma((NH, NGY)), dma((NH, NGY)),
    ]
    result, weights = pl.pallas_call(
        kernel,
        out_shape=(
            jax.ShapeDtypeStruct(field, BF),
            jax.ShapeDtypeStruct((2,), F32),
        ),
        in_specs=[hbm, vmem, vmem, vmem, hbm, smem, hbm, hbm, hbm, vmem, vmem, hbm, hbm, hbm, hbm],
        out_specs=(hbm, smem),
        scratch_shapes=scratch,
        compiler_params=pltpu.CompilerParams(
            collective_id=0, has_side_effects=True, vmem_limit_bytes=60 * 1024 * 1024),
        cost_estimate=pl.CostEstimate(
            flops=10_000_000_000, bytes_accessed=40_000_000, transcendentals=5_000_000),
    )(forcing, lift_weight.T, lift_bias.reshape(1, C), point_weight,
      jnp.transpose(spectral_weight, (0, 2, 1, 3)), mixing,
      iterate, prev_iterate, prev_residual, ex, ix, kz, kzi, ky, kyi)
    return result, weights


def solution(mesh):
    in_specs = (
        P(None, "gy", "gz", None),
        P(),
        P(),
        P(),
        P("gz", "gy", None, None),
        P(),
        P(None, "gy", "gz", None),
        P(None, "gy", "gz", None),
        P(None, "gy", "gz", None),
    )
    out_specs = (P(None, "gy", "gz", None), P())
    return jax.shard_map(shards, mesh=mesh, in_specs=in_specs, out_specs=out_specs, check_vma=False)
```
